256 devices in a mesh: gx: 8 (over z), gy: 32 (over x, y, core).
Axes of the slice: x: 4, y: 4, z: 8, core: 2. Of those that a mesh axis runs over, the one named last changes fastest.
Arguments:
- rhs: float32 [4, 128, 131072], P(None, None, ('gx', 'gy')), may hold values from -6 to 6
- offsets: float32 [3, 128, 131072], P(None, None, ('gx', 'gy')), may hold values from -4 to 4
- lengths: float32 [131072], P(('gx', 'gy')), may hold values from 1 to 4
- bucket: int32 [131072, 1], P(('gx', 'gy')), may hold values from 0 to 7; in each aligned block of 512 rows (0 to 511, 512 to 1023, ...) at most 128 rows name the same one
- attach: int32 [131072], P(('gx', 'gy')), may hold values from 0 to 2047
- operator: float32 [8, 512, 512], P('gx'), may hold values from -0.25 to 0.25
- inverse: float32 [8, 512, 512], P('gx'), as said below
- mobility: float32 [36, 16384], P(None, ('gx', 'gy')), may hold values from -2.5 to 2.5
Outputs:
- velocity: float32 [4, 128, 131072], P(None, None, ('gx', 'gy'))
The draws below stay inside these ranges and needn't reach their ends.
Inputs may be any that keep to these rules, and one draw needn't show every extreme that they name: Bucket b owns fibers of 16 * 2^(b mod 4) nodes. Among the 512 fibers of one device no bucket has more than 128, and in every draw some bucket has exactly 128 there. `inverse`: identity plus a dense full-rank part.
All inputs are finite; a program needn't handle non-finite values.
Results may differ from the reference program's by a relative error of at most 0.0003.
Values sent between devices are 32-bit elements; how exact they have to be, the bound alone decides.
A program may use at most 64 MiB of HBM per device.

```python
import math
import jax
import jax.numpy as jnp
import numpy as np
from jax import lax

NODE_MIN = 16
NODE_MAX = 128
ITERS = 4
FIB_DEV = 512
CEN_DEV = 64
CEN_SLAB = 2048
FIBERS = 131072
CENTROS = 16384
N_GX = 8
N_GY = 32


def draw_inverse(key, part):
    order_size = 4 * NODE_MAX
    noise = jax.random.normal(key, (N_GX, order_size, order_size), jnp.float32)
    return jnp.eye(order_size, dtype=jnp.float32)[None] + 0.4 * noise / math.sqrt(order_size)


def set_ends(drawn, key, smallest, largest):
    place = [jax.random.randint(jax.random.fold_in(key, axis), (), 0, length) for axis, length in enumerate(drawn.shape)]
    longest = drawn.shape.index(max(drawn.shape))
    next_to = place[:longest] + [(place[longest] + 1) % drawn.shape[longest]] + place[longest + 1:]
    return drawn.at[tuple(place)].set(smallest).at[tuple(next_to)].set(largest)


def block_levels(own_key, shape, shards, low, largest):
    factor_of = 1.0
    for dim, parts in shards:
        steps = jax.random.uniform(jax.random.fold_in(jax.random.fold_in(own_key, 6), dim), (parts,), jnp.float32, low / len(shards), largest / len(shards))
        factor_of = factor_of * jnp.repeat(jnp.exp(steps), shape[dim] // parts).reshape((-1,) + (1,) * (len(shape) - 1 - dim))
    return factor_of


def deal_out(own_key, own, number, rows, count, top, most, slope):
    ranking = jax.random.permutation(own_key, count)
    heavy_load, common = shares(count, rows * top, most, slope, True), shares(count, rows * top, most, slope, False)
    places = jnp.arange(count)

    def named(sizes, offset_by):
        used = int((sizes > 0).sum())
        fixed = max(1, used // 4)
        moved = fixed + (places - fixed + offset_by * (used - fixed)) % max(1, count - fixed)
        return jnp.zeros((count,), jnp.int32).at[ranking[jnp.where(places < fixed, places, moved)]].set(jnp.asarray(sizes, jnp.int32))

    sizes = jnp.where(number % 4 == 0, named(heavy_load, number // 4), named(common, number - number // 4 - 1))
    mixed = jax.random.permutation(jax.random.fold_in(own, 3), count)
    source_of, sink = mixed[0:count // 2 * 2:2], mixed[1:count // 2 * 2:2]
    slack = jnp.minimum(sizes[source_of] - 1, most - sizes[sink]) // 2
    slack = jnp.where((source_of == ranking[0]) | (sink == ranking[0]) | (sizes[sink] == 0), 0, jnp.maximum(slack, 0))
    moved = jax.random.randint(jax.random.fold_in(own, 4), (count // 2,), 0, 1 << 20) % (slack + 1)
    sizes = sizes.at[source_of].add(-moved).at[sink].add(moved)
    members = jnp.searchsorted(jnp.cumsum(sizes), jnp.arange(rows * top), side="right").astype(jnp.int32)
    listing = members.reshape(top, rows).T
    listing = listing[jax.random.permutation(jax.random.fold_in(own, 1), rows)]
    offset_by = jax.random.randint(jax.random.fold_in(own, 2), (rows, 1), 0, top)
    return jnp.take_along_axis(listing, (jnp.arange(top)[None, :] + offset_by) % top, axis=1)


def shares(amount, total, bound, lean, full):
    portions = [(1 << 20) // math.isqrt(grade ** lean) + 1 for grade in range(1, amount + 1)]
    largest = bound if full else min(bound, max(-(-total // amount), total * portions[0] // sum(portions)))
    least = 1 if total - largest >= amount - 1 else 0
    holding, spare = [largest] + [least] * (amount - 1), total - largest - least * (amount - 1)
    while spare > 0:
        free = [i for i in range(1, amount) if holding[i] < largest] or [i for i in range(1, amount) if holding[i] < bound]
        pool, left = sum([portions[i] for i in free]), spare
        for i in free:
            addition = min(bound - holding[i], max(1, left * portions[i] // pool), spare)
            holding[i] = holding[i] + addition
            spare = spare - addition
    return np.array(holding)


def gaussian(stream_key, dims, deviation, limit, split=(), kind=jnp.bfloat16):
    loudness = block_levels(stream_key, dims, split, -0.22, 0.18) if split else 1.0
    drawn = jax.random.normal(stream_key, dims, jnp.float32) * deviation * loudness
    return jnp.minimum(jnp.maximum(drawn, -limit), limit).astype(kind)


def setup_inputs(seed: int = 0) -> dict:
    splits = jax.random.split(jax.random.key(seed), 9)
    rhs = gaussian(splits[0], (4, NODE_MAX, FIBERS), 1.0, 6.0, ((2, 256),), jnp.float32)
    offsets = gaussian(splits[1], (3, NODE_MAX, FIBERS), 0.6, 4.0, ((2, 256),), jnp.float32)
    lengths = jnp.clip(jnp.exp(math.log(4.0) - 1.3862944 * jax.random.uniform(splits[2], (FIBERS,), jnp.float32) ** block_levels(splits[2], (FIBERS,), ((0, 256),), -0.2, 0.2)), 1.0, 4.0)
    bucket_keys = jax.random.split(jax.random.fold_in(splits[3], 1), FIBERS // FIB_DEV)
    bucket_turns = jax.random.permutation(jax.random.fold_in(splits[3], 3), FIBERS // FIB_DEV)
    bucket = jax.vmap(lambda own, number: deal_out(jax.random.fold_in(splits[3], 2), own, number, FIB_DEV, N_GX, 1, FIB_DEV // 4, 2))(bucket_keys, bucket_turns).reshape((FIBERS, 1))
    attach = set_ends(jax.random.randint(splits[4], (FIBERS,), 0, CEN_SLAB), jax.random.fold_in(splits[4], 1), 0, CEN_SLAB - 1).astype(jnp.int32)
    operator = gaussian(splits[5], (N_GX, 4 * NODE_MAX, 4 * NODE_MAX), (4 * NODE_MAX) ** -0.5, 0.25, ((0, 8),), jnp.float32)
    inverse = draw_inverse(jax.random.fold_in(splits[8], 71), 0)
    mobility = gaussian(splits[7], (36, CENTROS), 6 ** -0.5, 2.5, ((1, 256),), jnp.float32)
    return {"rhs": rhs, "offsets": offsets, "lengths": lengths, "bucket": bucket, "attach": attach, "operator": operator, "inverse": inverse, "mobility": mobility}


PRECISE = lax.Precision.HIGHEST


def couple(geometry, iterate):
    along = jnp.sum(geometry * iterate[:3], axis=0)
    transverse = geometry * (along + iterate[3])[None]
    return 0.15 * jnp.concatenate([transverse, along[None]], axis=0)


def reference(rhs, offsets, lengths, bucket, attach, operator, inverse, mobility):
    fibers = rhs.shape[2]
    nodes_max = rhs.shape[1]
    target = bucket[:, 0].astype(jnp.int32)
    levels = target % 4
    counts = NODE_MIN * jnp.left_shift(jnp.ones_like(levels), levels)
    fiber_index = jnp.arange(fibers, dtype=jnp.int32)
    node_mask = (jnp.arange(nodes_max, dtype=jnp.int32)[:, None] < counts[None, :]).astype(jnp.float32)
    geometry = offsets * node_mask
    coefficient = 0.3 / lengths
    capacity = (FIB_DEV // 4) * N_GX * N_GY
    solution = jnp.zeros((4, nodes_max, fibers), jnp.float32)
    for bucket_id in range(N_GX):
        node_count = NODE_MIN * 2 ** (bucket_id % 4)
        order_size = 4 * node_count
        chosen = target == bucket_id
        position = jnp.cumsum(chosen.astype(jnp.int32)) - 1
        position = jnp.where(chosen, position, capacity).astype(jnp.int32)
        slot_fiber = jnp.full((capacity,), fibers, jnp.int32).at[position].set(fiber_index, mode="drop")
        live_slot = (slot_fiber < fibers).astype(jnp.float32)
        picked = jnp.minimum(slot_fiber, fibers - 1).astype(jnp.int32)
        source = rhs[:, :node_count][:, :, picked] * live_slot
        geometry_b = geometry[:, :node_count][:, :, picked]
        factor = coefficient[picked] * live_slot
        stiffness = operator[bucket_id].reshape(4, nodes_max, 4, nodes_max)[:, :node_count, :, :node_count].reshape(order_size, order_size)
        inverse_b = inverse[bucket_id].reshape(4, nodes_max, 4, nodes_max)[:, :node_count, :, :node_count].reshape(order_size, order_size)

        def multiply(matrix, vector):
            product = jnp.dot(matrix, vector.reshape(order_size, capacity), precision=PRECISE)
            return product.reshape(4, node_count, capacity)

        iterate = multiply(inverse_b, source)
        for sweep in range(ITERS):
            iterate = multiply(inverse_b, source - factor * multiply(stiffness, iterate) - couple(geometry_b, iterate))
        solution = solution.at[:, :node_count, slot_fiber].set(iterate, mode="drop")
    weight = lengths / counts.astype(jnp.float32)
    clamp_force = weight * jnp.sum(solution[:3], axis=1)
    torque = weight * jnp.sum(jnp.cross(geometry, solution[:3], axis=0), axis=1)
    wrench = jnp.concatenate([clamp_force, torque], axis=0)
    slab_index = fiber_index // (FIB_DEV * N_GY)
    centre = (slab_index * (CEN_DEV * N_GY) + attach).astype(jnp.int32)
    wrench_table = jnp.zeros((6, CEN_DEV * N_GY * N_GX), jnp.float32).at[:, centre].add(wrench)
    motion = jnp.sum(mobility.reshape(6, 6, -1) * wrench_table[None], axis=1)
    moving = motion[:, centre]
    rigid_motion = moving[:3, None, :] + jnp.cross(moving[3:, None, :], geometry, axis=0)
    return jnp.concatenate([solution[:3] + rigid_motion * node_mask[None], solution[3:]], axis=0)
```

```python
import jax
import jax.numpy as jnp
from jax import lax
from jax.experimental import pallas as pl
from jax.experimental.pallas import tpu as pltpu
from jax.sharding import PartitionSpec as P

ITERS = 4
FIB = 512
CEN = 64
MESH = pl.DeviceIdType.MESH
F32, BF16 = jnp.float32, jnp.bfloat16
NODES = (16, 32, 64, 128)


def dot_nn(a, b):
    return lax.dot_general(a, b, (((1,), (0,)), ((), ())), preferred_element_type=F32)


def dot_nt(a, b):
    return lax.dot_general(a, b, (((1,), (1,)), ((), ())), preferred_element_type=F32)


def split2(x):
    hi = x.astype(BF16)
    return hi, (x - hi.astype(F32)).astype(BF16)


def stack3(x):
    hi = x.astype(BF16).astype(F32)
    rest = x - hi
    mid = rest.astype(BF16).astype(F32)
    return jnp.concatenate([hi, mid, rest - mid, jnp.zeros_like(x)], axis=0).astype(BF16)


def sum3(r):
    return r[0:8] + r[8:16] + r[16:24]


def product(matrix, x, pad=None):
    hi, lo = split2(x)
    right = jnp.concatenate([hi, lo], axis=1)
    if pad is not None:
        zeros = jnp.zeros_like(right)
        right = jnp.concatenate([right, zeros] if pad == 0 else [zeros, right], axis=0)
    r = dot_nn(matrix, right)
    m = r.shape[0] // 2
    return r[:m, :128] + (r[:m, 128:] + r[m:, :128])


def kernel(
    rhs_h, off_h, len_ref, bucket_ref, attach_ref, op_h, inv_h, mob_ref, out_ref,
    rhs, off, gs, gp, gk, st, m3, m2, m1, m0, mt, xhl, onehot,
    src3, src2, src1, src0, geo3, geo2, geo1, geo0, x3, x2, x1, x0, fac, wr,
    tab, got, mot, mob,
    in_sem, st_sem, own_sem, zs_sem, zp_sem, zk_sem, zrs_sem, zrp_sem, zrk_sem,
    ring_s, ring_r, t_s, t_r, mo_s, mo_r, mob_s, mob_r,
):
    z = lax.axis_index("gx")
    g = lax.axis_index("gy")
    x, y, c = lax.div(g, 8), lax.rem(lax.div(g, 2), 4), lax.rem(g, 2)
    u, v = x + c * (y - x), y + c * (x - y)
    r = c * 16 + v * 4 + u
    level, bb = lax.rem(z, 4), lax.div(z, 4)

    def plane(vv, uu):
        xx, yy = uu + c * (vv - uu), vv + c * (uu - vv)
        return (z, (xx * 4 + yy) * 2 + c)

    u_up, u_down = lax.rem(u + 1, 4), lax.rem(u + 3, 4)
    v_up, v_down = lax.rem(v + 1, 4), lax.rem(v + 3, 4)
    sib = (z, g + 1 - 2 * c)

    def greet_line(d, n):
        pl.semaphore_signal(
            pltpu.get_barrier_semaphore(), inc=1, device_id=(lax.rem(z + d, 8), g), device_id_type=MESH
        )
        return n

    def greet_plane(d, n):
        pl.semaphore_signal(
            pltpu.get_barrier_semaphore(), inc=1, device_id=(z, lax.rem(g + d, 32)), device_id_type=MESH
        )
        return n

    lax.fori_loop(1, 8, greet_line, 0)
    lax.fori_loop(1, 32, greet_plane, 0)

    load_rhs = pltpu.make_async_copy(rhs_h, rhs, in_sem.at[0])
    load_off = pltpu.make_async_copy(off_h, off, in_sem.at[1])
    load_rhs.start()
    load_off.start()

    lane = lax.broadcasted_iota(jnp.int32, (8, 128), 1)

    def stage(row):
        row = pl.multiple_of(row, 8)
        a = pltpu.make_async_copy(inv_h.at[0, pl.ds(row, 8)], st.at[0], st_sem.at[0])
        b = pltpu.make_async_copy(op_h.at[0, pl.ds(row, 8)], st.at[1], st_sem.at[1])
        a.start()
        b.start()
        a.wait()
        b.wait()

    row3 = pl.multiple_of(r * 16, 16)

    @pl.when(level == 2)
    def _():
        stage(lax.div(r, 8) * 128 + lax.rem(r, 8) * 8)
        for m in range(2):
            for h in range(2):
                left = st[m, :, 256 * h : 256 * h + 128]
                right = st[m, :, 256 * h + 128 : 256 * h + 256]
                gs[c, v, u, bb, 2 + 2 * m + h] = jnp.where(lane < 64, left, pltpu.roll(right, 64, 1))

    @pl.when(level == 1)
    def _():
        q = lax.rem(r, 16)
        stage(lax.div(q, 4) * 128 + lax.rem(q, 4) * 8)
        total = jnp.zeros((8, 128), F32)
        for cc in range(4):
            part = jnp.where(c == 0, st[0, :, 128 * cc : 128 * cc + 128], st[1, :, 128 * cc : 128 * cc + 128])
            part = pltpu.roll(part, 32 * cc, 1) if cc else part
            total = jnp.where((lane >= 32 * cc) & (lane < 32 * cc + 32), part, total)
        gs[c, v, u, bb, 1] = total

    @pl.when(level == 0)
    def _():
        q = lax.rem(r, 8)
        stage(lax.div(q, 2) * 128 + lax.rem(q, 2) * 8)
        total = jnp.zeros((8, 128), F32)
        for m in range(2):
            for cc in range(4):
                at = 64 * m + 16 * cc
                part = st[m, :, 128 * cc : 128 * cc + 128]
                part = pltpu.roll(part, at, 1) if at else part
                total = jnp.where((lane >= at) & (lane < at + 16), part, total)
        gs[c, v, u, bb, 0] = total

    own_p = pltpu.make_async_copy(inv_h.at[0, pl.ds(row3, 16)], gp.at[c, v, u, bb], own_sem.at[0])
    own_k = pltpu.make_async_copy(op_h.at[0, pl.ds(row3, 16)], gk.at[c, v, u, bb], own_sem.at[1])

    @pl.when(level == 3)
    def _():
        own_p.start()
        own_k.start()

    pl.semaphore_wait(pltpu.get_barrier_semaphore(), 38)

    def line_copy(src, dst, sends, recv, d):
        return pltpu.make_async_remote_copy(
            src_ref=src, dst_ref=dst, send_sem=sends.at[d - 1], recv_sem=recv,
            device_id=(lax.rem(z + d, 8), g), device_id_type=MESH,
        )

    def small_slot(lev, b):
        first, count = ((0, 1), (1, 1), (2, 4))[lev]
        return gs.at[c, v, u, b, pl.ds(first, count)]

    def line_small(lev, b, d):
        slot = small_slot(lev, b)
        return line_copy(slot, slot, zs_sem, zrs_sem.at[lev, b], d)

    def line_p(b, d):
        return line_copy(inv_h.at[0, pl.ds(row3, 16)], gp.at[c, v, u, b], zp_sem, zrp_sem.at[b], d)

    def line_k(b, d):
        return line_copy(op_h.at[0, pl.ds(row3, 16)], gk.at[c, v, u, b], zk_sem, zrk_sem.at[b], d)

    for lev in range(3):

        @pl.when(level == lev)
        def _(lev=lev):
            for d in (4, 3, 5, 2, 6, 1, 7):
                line_small(lev, bb, d).start()

    @pl.when(level == 3)
    def _():
        for d in (4, 3, 5, 2, 6, 1, 7):
            line_p(bb, d).start()
        for d in (4, 3, 5, 2, 6, 1, 7):
            line_k(bb, d).start()

    def send(k, i, src, to):
        return pltpu.make_async_remote_copy(
            src_ref=src, dst_ref=src, send_sem=ring_s.at[k, i], recv_sem=ring_r.at[k, i],
            device_id=to, device_id_type=MESH,
        )

    def steps_of(k, b):
        v_far = lax.rem(v + 2, 4)
        return {
            "a": [send(k, 0, b.at[c, v, u], plane(v, u_up)), send(k, 1, b.at[c, v, u], plane(v, u_down))],
            "b": [send(k, 2, b.at[c, v, u_down, 0], plane(v, u_up)), send(k, 3, b.at[c, v, u_up, 1], plane(v, u_down))],
            "c": [send(k, 4, b.at[c, v], plane(v_up, u)), send(k, 5, b.at[c, v], plane(v_down, u))],
            "d": [
                send(k, 6, b.at[c, v_down, pl.ds(0, 2)], plane(v_up, u)),
                send(k, 7, b.at[c, v_up, pl.ds(2, 2)], plane(v_down, u)),
            ],
            "s0": [send(k, 8, b.at[c, v], sib)],
            "s1": [send(k, 9, b.at[c, v_down], sib), send(k, 10, b.at[c, v_up], sib)],
            "s2": [send(k, 11, b.at[c, v_far], sib)],
        }

    kinds = [steps_of(0, gs), steps_of(1, gp), steps_of(2, gk)]

    def go(k, *names):
        for name in names:
            for copy in kinds[k][name]:
                copy.start()

    def arrived(k, *names):
        for name in names:
            for copy in kinds[k][name]:
                copy.wait_recv()

    def from_line(k):
        if k == 0:
            for lev in range(3):
                for b in range(2):

                    @pl.when(z != 4 * b + lev)
                    def _(lev=lev, b=b):
                        line_small(lev, b, 1).wait_recv()

            return
        line, own = ((line_p, own_p), (line_k, own_k))[k - 1]
        for b in range(2):

            @pl.when(z != 4 * b + 3)
            def _(b=b):
                line(b, 1).wait_recv()

        @pl.when(level == 3)
        def _():
            own.wait()

    bucket = bucket_ref[...]
    own_level = jnp.bitwise_and(bucket, 3)
    counts = jnp.left_shift(jnp.full((1, FIB), 16, jnp.int32), own_level)
    marks = (lax.broadcasted_iota(jnp.int32, (16, FIB), 0) == bucket).astype(F32)
    before = lax.broadcasted_iota(jnp.int32, (FIB, FIB), 0) < lax.broadcasted_iota(jnp.int32, (FIB, FIB), 1)
    ranks = dot_nn(marks.astype(BF16), before.astype(F32).astype(BF16))
    rank = jnp.sum(ranks * marks, axis=0, keepdims=True)
    column = (own_level * 256 + jnp.right_shift(bucket, 2) * 128).astype(F32) + rank
    for i in range(8):
        place = (lax.broadcasted_iota(jnp.int32, (128, FIB), 0) + 128 * i).astype(F32)
        mt[128 * i : 128 * (i + 1), :] = (place == column).astype(F32).astype(BF16)

    load_rhs.wait()
    load_off.wait()
    for cc in range(7):
        hi, lo = split2(rhs[cc] if cc < 4 else off[cc - 4])
        xhl[256 * cc : 256 * cc + 128, :] = hi
        xhl[256 * cc + 128 : 256 * cc + 256, :] = lo

    srcs, geos, xs = (src0, src1, src2, src3), (geo0, geo1, geo2, geo3), (x0, x1, x2, x3)

    def regroup(lev):
        n = NODES[lev]
        slots = mt[256 * lev : 256 * lev + 256, :]
        if lev == 3:
            left = xhl[...]
        else:
            left = jnp.concatenate([xhl[128 * i : 128 * i + n, :] for i in range(14)], axis=0)
        moved = dot_nt(left, slots)
        for cc in range(7):
            value = moved[2 * n * cc : 2 * n * cc + n] + moved[2 * n * cc + n : 2 * n * cc + 2 * n]
            if cc < 4:
                srcs[lev][n * cc : n * cc + n, :] = value
            else:
                geos[lev][n * (cc - 4) : n * (cc - 4) + n, :] = value

    from_line(0)
    go(0, "a")

    coefficient = 0.3 / len_ref[...]
    hi = coefficient.astype(BF16).astype(F32)
    terms = jnp.where(lax.broadcasted_iota(jnp.int32, (16, FIB), 0) < 8, hi, coefficient - hi)
    factors = dot_nt(terms.astype(BF16), mt[...])
    fac[...] = factors[0:8] + factors[8:16]

    regroup(3)
    from_line(1)
    go(1, "a")
    arrived(0, "a")
    go(0, "b")
    regroup(2)
    from_line(2)
    go(2, "a")
    arrived(1, "a")
    go(1, "b")
    arrived(0, "b")
    go(0, "c", "s0")
    regroup(1)
    regroup(0)
    arrived(2, "a")
    go(2, "b")
    arrived(1, "b")
    go(1, "c", "s0")
    arrived(0, "c")
    go(0, "d", "s1")

    attach = attach_ref[...]

    def mark(i, n):
        start = pl.multiple_of(i * 256, 256)
        named = lax.broadcasted_iota(jnp.int32, (256, FIB), 0) + start
        onehot[pl.ds(start, 256), :] = (named == attach).astype(F32).astype(BF16)
        return n

    lax.fori_loop(0, 8, mark, 0)
    wide = jnp.concatenate([mob_ref[...], jnp.zeros((36, 64), F32)], axis=1)
    mob[c, 0:36, :] = jnp.where(c == 0, wide, pltpu.roll(wide, 64, 1))
    send_mob = pltpu.make_async_remote_copy(
        src_ref=mob.at[c], dst_ref=mob.at[c], send_sem=mob_s, recv_sem=mob_r, device_id=sib, device_id_type=MESH
    )
    send_mob.start()

    arrived(2, "b")
    go(2, "c", "s0")
    arrived(0, "d")
    go(0, "s2")

    def split_into(ref, i, matrix):
        hi, lo = split2(matrix)
        m = matrix.shape[0]
        ref[i, 0:m, :] = hi
        ref[i, m : 2 * m, :] = lo

    def sweep(lev, stiff, inverse):
        n = NODES[lev]
        held, geo, start = xs[lev], geos[lev], srcs[lev]
        for b in range(2):
            cols = slice(128 * b, 128 * b + 128)
            f = fac[0:1, 256 * lev + 128 * b : 256 * lev + 128 * b + 128]
            now = held[:, cols]
            pulled = stiff(b, now)
            o = [geo[n * i : n * i + n, cols] for i in range(3)]
            w = [now[n * i : n * i + n] for i in range(4)]
            along = 0.15 * (o[0] * w[0] + o[1] * w[1] + o[2] * w[2])
            across = along + 0.15 * w[3]
            held[:, cols] = start[:, cols] - f * pulled - jnp.concatenate(
                [o[0] * across, o[1] * across, o[2] * across, along], axis=0
            )
        for b in range(2):
            cols = slice(128 * b, 128 * b + 128)
            held[:, cols] = inverse(b, held[:, cols])

    arrived(0, "s0", "s1", "s2")
    for b in range(2):
        split_into(m0, b, gs[0, 0:2, :, b, 0].reshape(64, 128))
        split_into(m1, b, gs[0, :, :, b, 1].reshape(128, 128))
        split_into(m1, 2 + b, gs[1, :, :, b, 1].reshape(128, 128))
        for m in range(2):
            left, right = gs[:, :, :, b, 2 + 2 * m].reshape(256, 128), gs[:, :, :, b, 3 + 2 * m].reshape(256, 128)
            split_into(m2, 2 * m + b, jnp.concatenate([left, right], axis=1))

    inverses = (
        lambda b, w: product(m0[b], w, 0),
        lambda b, w: product(m1[b], w),
        lambda b, w: product(m2[b], w),
        lambda b, w: product(m3[b], w),
    )
    stiffs = (
        lambda b, w: product(m0[b], w, 1),
        lambda b, w: product(m1[2 + b], w),
        lambda b, w: product(m2[2 + b], w),
        lambda b, w: product(m3[2 + b], w),
    )

    def begin(lev):
        for b in range(2):
            cols = slice(128 * b, 128 * b + 128)
            xs[lev][:, cols] = inverses[lev](b, srcs[lev][:, cols])

    def small_sweeps(i, n):
        for lev in range(3):
            sweep(lev, stiffs[lev], inverses[lev])
        return n

    for lev in range(3):
        begin(lev)
    arrived(1, "c")
    go(1, "d", "s1")
    lax.fori_loop(0, 2, small_sweeps, 0)
    arrived(2, "c")
    go(2, "d", "s1")
    arrived(1, "d")
    go(1, "s2")
    lax.fori_loop(0, 2, small_sweeps, 0)

    arrived(1, "s0", "s1", "s2")
    for b in range(2):
        split_into(m3, b, gp[:, :, :, b].reshape(512, 512))
    begin(3)
    arrived(2, "d")
    go(2, "s2")
    arrived(2, "s0", "s1", "s2")
    for b in range(2):
        split_into(m3, 2 + b, gk[:, :, :, b].reshape(512, 512))

    def large_sweeps(i, n):
        sweep(3, stiffs[3], inverses[3])
        return n

    lax.fori_loop(0, ITERS, large_sweeps, 0)

    wr[...] = jnp.zeros_like(wr)
    for lev in range(4):
        n = NODES[lev]
        o = [geos[lev][n * i : n * i + n, :] for i in range(3)]
        w = [xs[lev][n * i : n * i + n, :] for i in range(3)]
        parts = w + [o[1] * w[2] - o[2] * w[1], o[2] * w[0] - o[0] * w[2], o[0] * w[1] - o[1] * w[0]]
        for i, part in enumerate(parts):
            wr[i : i + 1, 256 * lev : 256 * lev + 256] = jnp.sum(part, axis=0, keepdims=True)
    weight = len_ref[...] / counts.astype(F32)
    wrench = sum3(dot_nn(stack3(wr[...]), mt[...])) * weight
    table = sum3(dot_nt(stack3(wrench), onehot[...]))
    for q in range(16):
        tab[q] = table[:, 128 * q : 128 * q + 128]
    got[g] = tab[lax.div(g, 2)]

    def give(d):
        to = lax.rem(g + d, 32)
        return pltpu.make_async_remote_copy(
            src_ref=tab.at[lax.div(to, 2)], dst_ref=got.at[g], send_sem=t_s.at[d - 1], recv_sem=t_r.at[d - 1],
            device_id=(z, to), device_id_type=MESH,
        )

    def give_start(d, n):
        give(d).start()
        return n

    def give_wait(d, n):
        give(d).wait()
        return n

    lax.fori_loop(1, 32, give_start, 0)

    for lev in (3, 2, 1, 0):
        n = NODES[lev]
        hi, lo = split2(xs[lev][...])
        moved = dot_nn(jnp.concatenate([hi, lo], axis=0), mt[256 * lev : 256 * lev + 256, :])
        for cc in range(4):
            value = moved[n * cc : n * cc + n] + moved[4 * n + n * cc : 4 * n + n * cc + n]
            if lev == 3:
                out_ref[cc] = value
            else:
                out_ref[cc, 0:n, :] += value

    send_mob.wait()
    lax.fori_loop(1, 32, give_wait, 0)
    total = got[0]
    for i in range(1, 32):
        total = total + got[i]
    pair = mob[0, 0:36, :] + mob[1, 0:36, :]
    own_mot = lax.div(g, 2)
    rows = []
    for k in range(6):
        row = pair[6 * k : 6 * k + 1] * total[0:1]
        for j in range(1, 6):
            row = row + pair[6 * k + j : 6 * k + j + 1] * total[j : j + 1]
        rows.append(row)
    mot[own_mot] = jnp.concatenate(rows + [jnp.zeros((2, 128), F32)], axis=0)

    def tell(d):
        to = lax.rem(own_mot + d, 16)
        return pltpu.make_async_remote_copy(
            src_ref=mot.at[own_mot], dst_ref=mot.at[own_mot], send_sem=mo_s.at[d - 1], recv_sem=mo_r.at[d - 1],
            device_id=(z, to * 2 + c), device_id_type=MESH,
        )

    def tell_start(d, n):
        tell(d).start()
        return n

    def tell_wait(d, n):
        tell(d).wait()
        return n

    lax.fori_loop(1, 16, tell_start, 0)

    for steps in kinds:
        for copies in steps.values():
            for copy in copies:
                copy.wait_send()
    for lev in range(3):

        @pl.when(level == lev)
        def _(lev=lev):
            for d in range(1, 8):
                line_small(lev, bb, d).wait_send()

    @pl.when(level == 3)
    def _():
        for d in range(1, 8):
            line_p(bb, d).wait_send()
            line_k(bb, d).wait_send()

    lax.fori_loop(1, 16, tell_wait, 0)
    motions = jnp.concatenate([mot[q] for q in range(16)], axis=1)
    moving = sum3(dot_nn(stack3(motions), onehot[...]))
    live = lax.broadcasted_iota(jnp.int32, (128, FIB), 0) < counts
    o = [off[i] for i in range(3)]
    for i in range(3):
        j, k = (i + 1) % 3, (i + 2) % 3
        turn = moving[3 + j : 4 + j] * o[k] - moving[3 + k : 4 + k] * o[j]
        out_ref[i] += jnp.where(live, moving[i : i + 1] + turn, 0.0)


def body(rhs, offsets, lengths, bucket, attach, operator, inverse, mobility):
    any_ref, vmem = pl.BlockSpec(memory_space=pl.ANY), pl.BlockSpec(memory_space=pltpu.VMEM)
    dma = pltpu.SemaphoreType.DMA
    scratch = [
        pltpu.VMEM((4, 128, FIB), F32), pltpu.VMEM((3, 128, FIB), F32),
        pltpu.VMEM((2, 4, 4, 2, 6, 8, 128), F32),
        pltpu.VMEM((2, 4, 4, 2, 16, 512), F32), pltpu.VMEM((2, 4, 4, 2, 16, 512), F32),
        pltpu.VMEM((2, 8, 512), F32),
        pltpu.VMEM((4, 1024, 512), BF16), pltpu.VMEM((4, 512, 256), BF16),
        pltpu.VMEM((4, 256, 128), BF16), pltpu.VMEM((2, 128, 128), BF16),
        pltpu.VMEM((1024, FIB), BF16), pltpu.VMEM((7 * 256, FIB), BF16), pltpu.VMEM((32 * CEN, FIB), BF16),
        *[pltpu.VMEM((4 * n, 256), F32) for n in NODES[::-1]],
        *[pltpu.VMEM((3 * n, 256), F32) for n in NODES[::-1]],
        *[pltpu.VMEM((4 * n, 256), F32) for n in NODES[::-1]],
        pltpu.VMEM((8, 1024), F32), pltpu.VMEM((8, 1024), F32),
        pltpu.VMEM((16, 8, 128), F32), pltpu.VMEM((32, 8, 128), F32), pltpu.VMEM((16, 8, 128), F32),
        pltpu.VMEM((2, 40, 128), F32),
        dma((2,)), dma((2,)), dma((2,)), dma((7,)), dma((7,)), dma((7,)), dma((3, 2)), dma((2,)), dma((2,)),
        dma((3, 12)), dma((3, 12)), dma((31,)), dma((31,)), dma((15,)), dma((15,)), dma, dma,
    ]
    return pl.pallas_call(
        kernel,
        out_shape=jax.ShapeDtypeStruct((4, 128, FIB), F32),
        in_specs=[any_ref, any_ref, vmem, vmem, vmem, any_ref, any_ref, vmem],
        out_specs=vmem,
        scratch_shapes=scratch,
        compiler_params=pltpu.CompilerParams(
            collective_id=0, has_side_effects=True, vmem_limit_bytes=48 * 2**20
        ),
    )(
        rhs, offsets, lengths.reshape(1, FIB), bucket.reshape(1, FIB), attach.reshape(1, FIB),
        operator, inverse, mobility,
    )


def solution(mesh):
    both = ("gx", "gy")
    in_specs = (
        P(None, None, both), P(None, None, both), P(both), P(both, None), P(both),
        P("gx", None, None), P("gx", None, None), P(None, both),
    )
    return jax.shard_map(body, mesh=mesh, in_specs=in_specs, out_specs=P(None, None, both), check_vma=False)
```

```python
import jax
import jax.numpy as jnp
from jax import lax
from jax.experimental import pallas as pl
from jax.experimental.pallas import tpu as pltpu
from jax.sharding import PartitionSpec as P

ITERS = 4
FIB = 512
CEN = 64
MESH = pl.DeviceIdType.MESH
F32, BF16 = jnp.float32, jnp.bfloat16
NODES = (16, 32, 64, 128)


def dot_nn(a, b):
    return lax.dot_general(a, b, (((1,), (0,)), ((), ())), preferred_element_type=F32)


def dot_nt(a, b):
    return lax.dot_general(a, b, (((1,), (1,)), ((), ())), preferred_element_type=F32)


def split2(x):
    hi = x.astype(BF16)
    return hi, (x - hi.astype(F32)).astype(BF16)


def stack3(x):
    hi = x.astype(BF16).astype(F32)
    rest = x - hi
    mid = rest.astype(BF16).astype(F32)
    return jnp.concatenate([hi, mid, rest - mid, jnp.zeros_like(x)], axis=0).astype(BF16)


def sum3(r):
    return r[0:8] + r[8:16] + r[16:24]


def product(matrix, x):
    hi, lo = split2(x)
    m = matrix.shape[0] // 2
    first = dot_nn(matrix[...], hi)
    return first[:m] + (first[m:] + dot_nn(matrix[0:m, :], lo))


def kernel(
    rhs_h, off_h, len_h, bucket_h, attach_h, op_h, inv_h, mob_h, out_ref,
    len_ref, bucket_ref, attach_ref, mob_ref, rhs, off, gs, gp, gk, st, sg,
    m3, m2, m1, m0, mt, xhl, onehot, slothot,
    f3, f2, f1, f0, t3, t2, t1, t0, x3, x2, x1, x0, b3, b2, b1, b0, wr, asl,
    tab, got, mot, mob,
    in_sem, st_sem, own_sem, z_sem, zr_sem,
    ring_s, ring_r, fib_s, fib_r, back_s, back_r, t_s, t_r, mo_s, mo_r, mob_s, mob_r,
):
    z = lax.axis_index("gx")
    g = lax.axis_index("gy")
    x, y, c = lax.div(g, 8), lax.rem(lax.div(g, 2), 4), lax.rem(g, 2)
    u, v = x + c * (y - x), y + c * (x - y)
    level, bb = lax.rem(z, 4), lax.div(z, 4)
    ub, vb = x + bb * (y - x), y + bb * (x - y)
    rb = vb * 4 + ub
    away = c + bb - 2 * c * bb

    def plane(vv, uu):
        xx, yy = uu + c * (vv - uu), vv + c * (uu - vv)
        return (z, (xx * 4 + yy) * 2 + c)

    u_up, u_down = lax.rem(u + 1, 4), lax.rem(u + 3, 4)
    v_up, v_down = lax.rem(v + 1, 4), lax.rem(v + 3, 4)
    sib = (z, g + 1 - 2 * c)
    barrier = pltpu.get_barrier_semaphore()
    for d in range(1, 8):
        zz = lax.rem(z + d, 8)
        pl.semaphore_signal(barrier, inc=1, device_id=(zz, g), device_id_type=MESH)
        pl.semaphore_signal(barrier, inc=1, device_id=(zz, g + 1 - 2 * c), device_id_type=MESH)
    for d in range(1, 32):
        pl.semaphore_signal(barrier, inc=1, device_id=(z, lax.rem(g + d, 32)), device_id_type=MESH)

    load_rhs, load_off, load_bucket, load_len, load_attach, load_mob = loads = [
        pltpu.make_async_copy(source, place, in_sem.at[i])
        for i, (source, place) in enumerate((
            (rhs_h, rhs), (off_h, off), (bucket_h, bucket_ref),
            (len_h, len_ref), (attach_h, attach_ref), (mob_h, mob_ref),
        ))
    ]

    def stage(row, count):
        row = pl.multiple_of(row, 8)

        @pl.when(c == 0)
        def _():
            pltpu.make_async_copy(inv_h.at[0, pl.ds(row, count)], st.at[pl.ds(0, count)], st_sem).start()

        @pl.when(c == 1)
        def _():
            pltpu.make_async_copy(op_h.at[0, pl.ds(row, count)], st.at[pl.ds(0, count)], st_sem).start()

        for i in (2, 3, 4, 0, 1, 5):
            loads[i].start()
        pltpu.make_async_copy(inv_h.at[0, pl.ds(row, count)], st.at[pl.ds(0, count)], st_sem).wait()

    def lanes_of(rows):
        return lax.broadcasted_iota(jnp.int32, (rows, 128), 1)

    q1, q0 = rb, lax.rem(rb, 8)
    row3 = pl.multiple_of(rb * 32, 32)

    @pl.when(level == 2)
    def _():
        stage(lax.div(rb, 4) * 128 + lax.rem(rb, 4) * 16, 16)
        for h in range(2):
            left = st[:, 256 * h : 256 * h + 128]
            right = st[:, 256 * h + 128 : 256 * h + 256]
            part = jnp.where(lanes_of(16) < 64, left, pltpu.roll(right, 64, 1))
            sg[2 * h] = part[0:8]
            sg[2 * h + 1] = part[8:16]

    def compact(width):
        lane = lanes_of(8)
        total = jnp.zeros((8, 128), F32)
        for i in range(4):
            part = st[0:8, 128 * i : 128 * i + 128]
            part = pltpu.roll(part, width * i, 1) if i else part
            total = jnp.where((lane >= width * i) & (lane < width * i + width), part, total)
        sg[0] = total

    @pl.when(level == 1)
    def _():
        stage(lax.div(q1, 4) * 128 + lax.rem(q1, 4) * 8, 8)
        compact(32)

    @pl.when(level == 0)
    def _():
        stage(lax.div(q0, 2) * 128 + lax.rem(q0, 2) * 8, 8)
        compact(16)

    @pl.when(level == 3)
    def _():
        for i in (2, 3, 4, 0, 1, 5):
            loads[i].start()

    pl.semaphore_wait(barrier, 45)

    def rows_of(lev, m):
        if lev == 3:
            return (inv_h, op_h)[m].at[0, pl.ds(row3, 32)], (gp, gk)[m].at[vb, ub]
        first, count = ((m, 1), (2 + m, 1), (4 + 4 * m, 4))[lev]
        return sg.at[pl.ds(0, count)], gs.at[vb, ub, pl.ds(first, count)]

    def line(lev, m, d):
        source, slot = rows_of(lev, m)
        return pltpu.make_async_remote_copy(
            src_ref=source, dst_ref=slot, send_sem=z_sem.at[d], recv_sem=zr_sem.at[lev, m],
            device_id=(lax.rem(z + d, 8), g - c + bb), device_id_type=MESH,
        )

    def to_sibling(lev, m):
        source, slot = rows_of(lev, m)
        return pltpu.make_async_remote_copy(
            src_ref=source, dst_ref=slot, send_sem=z_sem.at[0], recv_sem=zr_sem.at[lev, m],
            device_id=sib, device_id_type=MESH,
        )

    def stays(lev, m):
        source, slot = rows_of(lev, m)
        return pltpu.make_async_copy(source, slot, own_sem.at[lev, m])

    for lev in range(4):
        for m in range(2):

            @pl.when((level == lev) & (c == m))
            def _(lev=lev, m=m):
                for d in (4, 3, 5, 2, 6, 1, 7):
                    line(lev, m, d).start()

            @pl.when((level == lev) & (c == m) & (bb != m))
            def _(lev=lev, m=m):
                to_sibling(lev, m).start()

            @pl.when((level == lev) & (c == m) & (bb == m))
            def _(lev=lev, m=m):
                stays(lev, m).start()

    def send(k, i, src, to):
        return pltpu.make_async_remote_copy(
            src_ref=src, dst_ref=src, send_sem=ring_s.at[k, i], recv_sem=ring_r.at[k, i],
            device_id=to, device_id_type=MESH,
        )

    def steps_of(k, b, half):
        return {
            "a": [send(k, 0, b.at[v, u], plane(v, u_up)), send(k, 1, b.at[v, u], plane(v, u_down))],
            "b": [
                send(k, 2, b.at[v, u_down, pl.ds(0, half)], plane(v, u_up)),
                send(k, 3, b.at[v, u_up, pl.ds(half, half)], plane(v, u_down)),
            ],
            "c": [send(k, 4, b.at[v], plane(v_up, u)), send(k, 5, b.at[v], plane(v_down, u))],
            "d": [
                send(k, 6, b.at[v_down, pl.ds(0, 2)], plane(v_up, u)),
                send(k, 7, b.at[v_up, pl.ds(2, 2)], plane(v_down, u)),
            ],
        }

    kinds = [steps_of(0, gs, 6), steps_of(1, gp, 16), steps_of(2, gk, 16)]

    def go(k, *names):
        for name in names:
            for copy in kinds[k][name]:
                copy.start()

    def arrived(k, *names):
        for name in names:
            for copy in kinds[k][name]:
                copy.wait_recv()

    def landing(lev, m):
        if lev == 3:
            slot = (gp, gk)[m].at[v, u]
        else:
            first, count = ((m, 1), (2 + m, 1), (4 + 4 * m, 4))[lev]
            slot = gs.at[v, u, pl.ds(first, count)]
        return pltpu.make_async_remote_copy(
            src_ref=slot, dst_ref=slot, send_sem=z_sem.at[0], recv_sem=zr_sem.at[lev, m],
            device_id=sib, device_id_type=MESH,
        )

    def from_line(k):
        for lev, m in (((0, 0), (0, 1), (1, 0), (1, 1), (2, 0), (2, 1)), ((3, 0),), ((3, 1),))[k]:

            @pl.when((z != 4 * c + lev) | (c != m))
            def _(lev=lev, m=m):
                landing(lev, m).wait_recv()

            @pl.when((z == 4 * c + lev) & (c == m))
            def _(lev=lev, m=m):
                stays(lev, m).wait()

    load_bucket.wait()
    load_len.wait()
    load_attach.wait()
    bucket = bucket_ref[...]
    own_level = jnp.bitwise_and(bucket, 3)
    counts = jnp.left_shift(jnp.full((1, FIB), 16, jnp.int32), own_level)
    marks = (lax.broadcasted_iota(jnp.int32, (16, FIB), 0) == bucket).astype(F32)
    before = lax.broadcasted_iota(jnp.int32, (FIB, FIB), 0) < lax.broadcasted_iota(jnp.int32, (FIB, FIB), 1)
    ranks = dot_nn(marks.astype(BF16), before.astype(F32).astype(BF16))
    rank = jnp.sum(ranks * marks, axis=0, keepdims=True)
    upper = jnp.right_shift(bucket, 2)
    other = upper + c - 2 * c * upper
    column = (own_level * 256 + other * 128).astype(F32) + rank
    for i in range(8):
        place = (lax.broadcasted_iota(jnp.int32, (128, FIB), 0) + 128 * i).astype(F32)
        mt[128 * i : 128 * (i + 1), :] = (place == column).astype(F32).astype(BF16)

    lengths = len_ref[...]
    attach = attach_ref[...]
    row = lax.broadcasted_iota(jnp.int32, (16, FIB), 0)
    which = jnp.bitwise_and(row, 7)
    extra = jnp.where(which == 0, 0.3 / lengths, jnp.where(which == 1, lengths / counts.astype(F32), 0.0))
    extra = jnp.where(which == 2, attach.astype(F32), extra)
    hi = extra.astype(BF16).astype(F32)
    xhl[1792:1808, :] = jnp.where(row < 8, hi, extra - hi).astype(BF16)

    load_rhs.wait()
    load_off.wait()
    for cc in range(7):
        hi, lo = split2(rhs[cc] if cc < 4 else off[cc - 4])
        xhl[256 * cc : 256 * cc + 128, :] = hi
        xhl[256 * cc + 128 : 256 * cc + 256, :] = lo

    fibers, leaving = (f0, f1, f2, f3), (t0, t1, t2, t3)
    xs, backs = (x0, x1, x2, x3), (b0, b1, b2, b3)

    def cross_over(lev):
        return pltpu.make_async_remote_copy(
            src_ref=leaving[lev], dst_ref=fibers[lev].at[c], send_sem=fib_s.at[lev], recv_sem=fib_r.at[lev],
            device_id=sib, device_id_type=MESH,
        )

    def come_back(lev):
        return pltpu.make_async_remote_copy(
            src_ref=xs[lev].at[1 - c], dst_ref=backs[lev], send_sem=back_s.at[lev], recv_sem=back_r.at[lev],
            device_id=sib, device_id_type=MESH,
        )

    def regroup(lev):
        n = NODES[lev]
        slots = mt[256 * lev : 256 * lev + 256, :]
        if lev == 3:
            left = xhl[...]
        else:
            left = jnp.concatenate([xhl[128 * i : 128 * i + n, :] for i in range(14)] + [xhl[1792:1808, :]], axis=0)
        moved = dot_nt(left, slots)
        for cc in range(7):
            value = moved[2 * n * cc : 2 * n * cc + n] + moved[2 * n * cc + n : 2 * n * cc + 2 * n]
            fibers[lev][c, n * cc : n * cc + n, :] = value[:, :128]
            leaving[lev][n * cc : n * cc + n, :] = value[:, 128:]
        value = moved[14 * n : 14 * n + 8] + moved[14 * n + 8 : 14 * n + 16]
        fibers[lev][c, 7 * n : 7 * n + 8, :] = value[:, :128]
        leaving[lev][7 * n : 7 * n + 8, :] = value[:, 128:]
        cross_over(lev).start()

    from_line(0)
    go(0, "a")
    for lev in (2, 1, 0):
        regroup(lev)
    arrived(0, "a")
    go(0, "b")
    from_line(1)
    go(1, "a")
    regroup(3)
    arrived(0, "b")
    go(0, "c")
    from_line(2)
    go(2, "a")
    arrived(1, "a")
    go(1, "b")

    def mark(i, n):
        start = pl.multiple_of(i * 256, 256)
        named = lax.broadcasted_iota(jnp.int32, (256, FIB), 0) + start
        onehot[pl.ds(start, 256), :] = (named == attach).astype(F32).astype(BF16)
        return n

    lax.fori_loop(0, 8, mark, 0)
    arrived(2, "a")
    go(2, "b")
    arrived(1, "b")
    go(1, "c")

    load_mob.wait()
    wide = jnp.concatenate([mob_ref[...], jnp.zeros((36, 64), F32)], axis=1)
    mob[c, 0:36, :] = jnp.where(c == 0, wide, pltpu.roll(wide, 64, 1))
    send_mob = pltpu.make_async_remote_copy(
        src_ref=mob.at[c], dst_ref=mob.at[c], send_sem=mob_s, recv_sem=mob_r, device_id=sib, device_id_type=MESH
    )
    send_mob.start()
    arrived(2, "b")
    go(2, "c")

    for lev in range(4):
        n = NODES[lev]
        cross_over(lev).wait_recv()
        for o in range(2):
            asl[0:1, 256 * lev + 128 * o : 256 * lev + 128 * o + 128] = fibers[lev][o, 7 * n + 2 : 7 * n + 3, :]
    arrived(0, "c")
    go(0, "d")
    named_by = asl[0:1, :]

    def mark_slots(i, n):
        start = pl.multiple_of(i * 128, 128)
        named = (lax.broadcasted_iota(jnp.int32, (128, 1024), 0) + start).astype(F32)
        slothot[pl.ds(start, 128), :] = (named == named_by).astype(F32).astype(BF16)
        return n

    lax.fori_loop(0, 16, mark_slots, 0)

    def split_into(ref, i, matrix):
        hi, lo = split2(matrix)
        m = matrix.shape[0]
        ref[i, 0:m, :] = hi
        ref[i, m : 2 * m, :] = lo

    mats = (m0, m1, m2, m3)

    def times(lev, i, w):
        if lev == 0:
            w = jnp.concatenate([w, jnp.zeros_like(w)], axis=0)
        return product(mats[lev].at[i], w)

    def both(ref, rows):
        return jnp.concatenate([ref[0, 0:rows, :], ref[1, 0:rows, :]], axis=1)

    def keep(lev, value):
        xs[lev][0] = value[:, :128]
        xs[lev][1] = value[:, 128:]

    def begin(lev):
        keep(lev, times(lev, 0, both(fibers[lev], 4 * NODES[lev])))

    def sweep(lev):
        n = NODES[lev]
        held, fib = xs[lev], fibers[lev]
        pulled = times(lev, 1, both(held, 4 * n))
        for o in range(2):
            f = fib[o, 7 * n : 7 * n + 1, :]
            a = [fib[o, n * (4 + i) : n * (5 + i), :] for i in range(3)]
            w = [held[o, n * i : n * i + n, :] for i in range(4)]
            along = 0.15 * (a[0] * w[0] + a[1] * w[1] + a[2] * w[2])
            across = along + 0.15 * w[3]
            for i in range(4):
                held[o, n * i : n * i + n, :] = (
                    fib[o, n * i : n * i + n, :]
                    - f * pulled[n * i : n * i + n, 128 * o : 128 * o + 128]
                    - (a[i] * across if i < 3 else along)
                )
        keep(lev, times(lev, 0, both(held, 4 * n)))

    def wrench_of(lev):
        n = NODES[lev]
        for o in range(2):
            a = [fibers[lev][o, n * (4 + i) : n * (5 + i), :] for i in range(3)]
            w = [xs[lev][o, n * i : n * i + n, :] for i in range(3)]
            weight = fibers[lev][o, 7 * n + 1 : 7 * n + 2, :]
            parts = w + [a[1] * w[2] - a[2] * w[1], a[2] * w[0] - a[0] * w[2], a[0] * w[1] - a[1] * w[0]]
            for i, part in enumerate(parts):
                wr[i : i + 1, 256 * lev + 128 * o : 256 * lev + 128 * o + 128] = (
                    jnp.sum(part, axis=0, keepdims=True) * weight
                )

    wr[...] = jnp.zeros_like(wr)
    arrived(0, "d")
    for m in range(2):
        split_into(m0, m, gs[0:2, :, m].reshape(64, 128))
        split_into(m1, m, gs[:, :, 2 + m].reshape(128, 128))
        left, right = [gs[:, :, 4 + 4 * m + 2 * h : 6 + 4 * m + 2 * h].reshape(256, 128) for h in range(2)]
        split_into(m2, m, jnp.concatenate([left, right], axis=1))
    for lev in range(3):
        begin(lev)
    arrived(1, "c")
    go(1, "d")

    def small_sweeps(i, n):
        for lev in range(3):
            sweep(lev)
        return n

    lax.fori_loop(0, 2, small_sweeps, 0)
    arrived(2, "c")
    go(2, "d")
    lax.fori_loop(0, 2, small_sweeps, 0)
    for lev in range(3):
        come_back(lev).start()
        wrench_of(lev)

    arrived(1, "d")
    split_into(m3, 0, gp[...].reshape(512, 512))
    begin(3)
    arrived(2, "d")
    split_into(m3, 1, gk[...].reshape(512, 512))

    def large_sweeps(i, n):
        sweep(3)
        return n

    lax.fori_loop(0, ITERS, large_sweeps, 0)
    come_back(3).start()
    wrench_of(3)
    table = sum3(dot_nt(stack3(wr[...]), slothot[...]))
    for q in range(16):
        tab[q] = table[:, 128 * q : 128 * q + 128]
    got[g] = tab[lax.div(g, 2)]
    for d in range(1, 32):
        to = lax.rem(g + d, 32)
        pltpu.make_async_remote_copy(
            src_ref=tab.at[lax.div(to, 2)], dst_ref=got.at[g], send_sem=t_s, recv_sem=t_r,
            device_id=(z, to), device_id_type=MESH,
        ).start()

    for lev in (2, 1, 0, 3):
        come_back(lev).wait_recv()
    for lev in (3, 2, 1, 0):
        n = NODES[lev]
        hi, lo = split2(jnp.concatenate([xs[lev][c], backs[lev][...]], axis=1))
        moved = dot_nn(jnp.concatenate([hi, lo], axis=0), mt[256 * lev : 256 * lev + 256, :])
        for cc in range(4):
            value = moved[n * cc : n * cc + n] + moved[4 * n + n * cc : 4 * n + n * cc + n]
            if lev == 3:
                out_ref[cc] = value
            else:
                out_ref[cc, 0:n, :] += value

    send_mob.wait()
    for lev in range(4):
        cross_over(lev).wait_send()
        come_back(lev).wait_send()
    for steps in kinds:
        for copies in steps.values():
            for copy in copies:
                copy.wait_send()
    for lev in range(4):
        for m in range(2):

            @pl.when((level == lev) & (c == m))
            def _(lev=lev, m=m):
                for d in range(1, 8):
                    line(lev, m, d).wait_send()

            @pl.when((level == lev) & (c == m) & (bb != m))
            def _(lev=lev, m=m):
                to_sibling(lev, m).wait_send()

    many = got.at[pl.ds(0, 31)]
    tables = pltpu.make_async_remote_copy(
        src_ref=many, dst_ref=many, send_sem=t_s, recv_sem=t_r, device_id=sib, device_id_type=MESH
    )
    tables.wait_send()
    tables.wait_recv()
    total = got[0]
    for i in range(1, 32):
        total = total + got[i]
    pair = mob[0, 0:36, :] + mob[1, 0:36, :]
    mine = lax.div(g, 2)
    rows = []
    for k in range(6):
        one = pair[6 * k : 6 * k + 1] * total[0:1]
        for j in range(1, 6):
            one = one + pair[6 * k + j : 6 * k + j + 1] * total[j : j + 1]
        rows.append(one)
    mot[mine] = jnp.concatenate(rows + [jnp.zeros((2, 128), F32)], axis=0)
    for d in range(1, 16):
        pltpu.make_async_remote_copy(
            src_ref=mot.at[mine], dst_ref=mot.at[mine], send_sem=mo_s, recv_sem=mo_r,
            device_id=(z, lax.rem(mine + d, 16) * 2 + c), device_id_type=MESH,
        ).start()
    most = mot.at[pl.ds(0, 15)]
    motions_come = pltpu.make_async_remote_copy(
        src_ref=most, dst_ref=most, send_sem=mo_s, recv_sem=mo_r, device_id=sib, device_id_type=MESH
    )
    motions_come.wait_send()
    motions_come.wait_recv()
    motions = jnp.concatenate([mot[q] for q in range(16)], axis=1)
    moving = sum3(dot_nn(stack3(motions), onehot[...]))
    live = lax.broadcasted_iota(jnp.int32, (128, FIB), 0) < counts
    a = [off[i] for i in range(3)]
    for i in range(3):
        j, k = (i + 1) % 3, (i + 2) % 3
        turn = moving[3 + j : 4 + j] * a[k] - moving[3 + k : 4 + k] * a[j]
        out_ref[i] += jnp.where(live, moving[i : i + 1] + turn, 0.0)


def body(rhs, offsets, lengths, bucket, attach, operator, inverse, mobility):
    hbm, vmem = pl.BlockSpec(memory_space=pltpu.HBM), pl.BlockSpec(memory_space=pltpu.VMEM)
    dma = pltpu.SemaphoreType.DMA
    scratch = [
        pltpu.VMEM((1, FIB), F32), pltpu.VMEM((1, FIB), jnp.int32), pltpu.VMEM((1, FIB), jnp.int32),
        pltpu.VMEM((36, CEN), F32),
        pltpu.VMEM((4, 128, FIB), F32), pltpu.VMEM((3, 128, FIB), F32),
        pltpu.VMEM((4, 4, 12, 8, 128), F32),
        pltpu.VMEM((4, 4, 32, 512), F32), pltpu.VMEM((4, 4, 32, 512), F32),
        pltpu.VMEM((16, 512), F32), pltpu.VMEM((4, 8, 128), F32),
        pltpu.VMEM((2, 1024, 512), BF16), pltpu.VMEM((2, 512, 256), BF16),
        pltpu.VMEM((2, 256, 128), BF16), pltpu.VMEM((2, 128, 128), BF16),
        pltpu.VMEM((1024, FIB), BF16), pltpu.VMEM((7 * 256 + 16, FIB), BF16), pltpu.VMEM((32 * CEN, FIB), BF16),
        pltpu.VMEM((32 * CEN, 1024), BF16),
        *[pltpu.VMEM((2, 7 * n + 8, 128), F32) for n in NODES[::-1]],
        *[pltpu.VMEM((7 * n + 8, 128), F32) for n in NODES[::-1]],
        *[pltpu.VMEM((2, 4 * n, 128), F32) for n in NODES[::-1]],
        *[pltpu.VMEM((4 * n, 128), F32) for n in NODES[::-1]],
        pltpu.VMEM((8, 1024), F32), pltpu.VMEM((8, 1024), F32),
        pltpu.VMEM((16, 8, 128), F32), pltpu.VMEM((32, 8, 128), F32), pltpu.VMEM((16, 8, 128), F32),
        pltpu.VMEM((2, 40, 128), F32),
        dma((6,)), dma, dma((4, 2)), dma((8,)), dma((4, 2)),
        dma((3, 8)), dma((3, 8)), dma((4,)), dma((4,)), dma((4,)), dma((4,)),
        dma, dma, dma, dma, dma, dma,
    ]
    return pl.pallas_call(
        kernel,
        out_shape=jax.ShapeDtypeStruct((4, 128, FIB), F32),
        in_specs=[hbm] * 8,
        out_specs=vmem,
        scratch_shapes=scratch,
        compiler_params=pltpu.CompilerParams(
            collective_id=0, has_side_effects=True, vmem_limit_bytes=60 * 2**20
        ),
    )(
        rhs, offsets, lengths.reshape(1, FIB), bucket.reshape(1, FIB), attach.reshape(1, FIB),
        operator, inverse, mobility,
    )


def solution(mesh):
    both = ("gx", "gy")
    in_specs = (
        P(None, None, both), P(None, None, both), P(both), P(both, None), P(both),
        P("gx", None, None), P("gx", None, None), P(None, both),
    )
    return jax.shard_map(body, mesh=mesh, in_specs=in_specs, out_specs=P(None, None, both), check_vma=False)
```

```python
import jax
import jax.numpy as jnp
from jax import lax
from jax.experimental import pallas as pl
from jax.experimental.pallas import tpu as pltpu
from jax.sharding import PartitionSpec as P

ITERS = 4
FIB = 512
CEN = 64
MESH = pl.DeviceIdType.MESH
F32, BF16 = jnp.float32, jnp.bfloat16
NODES = (16, 32, 64, 128)


def dot_nn(a, b):
    return lax.dot_general(a, b, (((1,), (0,)), ((), ())), preferred_element_type=F32)


def dot_nt(a, b):
    return lax.dot_general(a, b, (((1,), (1,)), ((), ())), preferred_element_type=F32)


def split2(x):
    hi = x.astype(BF16)
    return hi, (x - hi.astype(F32)).astype(BF16)


def product(matrix, x):
    hi, lo = split2(x)
    m = matrix.shape[0] // 2
    first = dot_nn(matrix[...], hi)
    return first[:m] + (first[m:] + dot_nn(matrix[0:m, :], lo))


def kernel(
    rhs_h, off_h, len_h, bucket_h, attach_h, op_h, inv_h, mob_h, sol_h, moving_ref,
    len_ref, bucket_ref, attach_ref, mob_ref, rhs, off, gs, gp, gk, gpz, gkz, st, sg,
    m3, m2, m1, m0, mt, xhl, fhot, shot, sol,
    f3, f2, f1, f0, t3, t2, t1, t0, x3, x2, x1, x0, b3, b2, b1, b0, wr, asl,
    tab, got, mot, mob,
    sol_sem, in_sem, st_sem, own_sem, z_sem, zz_sem, zr_sem,
    ring_s, ring_r, fib_s, fib_r, back_s, back_r, t_s, t_r, mo_s, mo_r, mob_s, mob_r,
):
    z = lax.axis_index("gx")
    g = lax.axis_index("gy")
    x, y, c = lax.div(g, 8), lax.rem(lax.div(g, 2), 4), lax.rem(g, 2)
    u, v = x + c * (y - x), y + c * (x - y)
    level, bb = lax.rem(z, 4), lax.div(z, 4)
    ub, vb = x + bb * (y - x), y + bb * (x - y)
    rb = vb * 4 + ub
    away = c + bb - 2 * c * bb

    def plane(vv, uu):
        xx, yy = uu + c * (vv - uu), vv + c * (uu - vv)
        return (z, (xx * 4 + yy) * 2 + c)

    u_up, u_down = lax.rem(u + 1, 4), lax.rem(u + 3, 4)
    v_up, v_down = lax.rem(v + 1, 4), lax.rem(v + 3, 4)
    u_far = lax.rem(u + 2, 4)
    sib = (z, g + 1 - 2 * c)
    barrier = pltpu.get_barrier_semaphore()
    for d in range(1, 8):
        zz = lax.rem(z + d, 8)
        pl.semaphore_signal(barrier, inc=1, device_id=(zz, g), device_id_type=MESH)
        pl.semaphore_signal(barrier, inc=1, device_id=(zz, g + 1 - 2 * c), device_id_type=MESH)
    for d in range(1, 32):
        pl.semaphore_signal(barrier, inc=1, device_id=(z, lax.rem(g + d, 32)), device_id_type=MESH)

    load_rhs, load_off, load_bucket, load_len, load_attach, load_mob = loads = [
        pltpu.make_async_copy(source, place, in_sem.at[i])
        for i, (source, place) in enumerate((
            (rhs_h, rhs), (off_h, off), (bucket_h, bucket_ref),
            (len_h, len_ref), (attach_h, attach_ref), (mob_h, mob_ref),
        ))
    ]

    def stage(row, count):
        row = pl.multiple_of(row, 8)

        @pl.when(c == 0)
        def _():
            pltpu.make_async_copy(inv_h.at[0, pl.ds(row, count)], st.at[pl.ds(0, count)], st_sem).start()

        @pl.when(c == 1)
        def _():
            pltpu.make_async_copy(op_h.at[0, pl.ds(row, count)], st.at[pl.ds(0, count)], st_sem).start()

        for i in (2, 3, 4, 0, 1, 5):
            loads[i].start()
        pltpu.make_async_copy(inv_h.at[0, pl.ds(row, count)], st.at[pl.ds(0, count)], st_sem).wait()

    def lanes_of(rows):
        return lax.broadcasted_iota(jnp.int32, (rows, 128), 1)

    q1, q0 = rb, lax.rem(rb, 8)
    row3 = pl.multiple_of(rb * 24, 8)

    @pl.when(level == 2)
    def _():
        stage(lax.div(rb, 4) * 128 + lax.rem(rb, 4) * 16, 16)
        for h in range(2):
            left = st[:, 256 * h : 256 * h + 128]
            right = st[:, 256 * h + 128 : 256 * h + 256]
            part = jnp.where(lanes_of(16) < 64, left, pltpu.roll(right, 64, 1))
            sg[2 * h] = part[0:8]
            sg[2 * h + 1] = part[8:16]

    def compact(width):
        lane = lanes_of(8)
        total = jnp.zeros((8, 128), F32)
        for i in range(4):
            part = st[0:8, 128 * i : 128 * i + 128]
            part = pltpu.roll(part, width * i, 1) if i else part
            total = jnp.where((lane >= width * i) & (lane < width * i + width), part, total)
        sg[0] = total

    @pl.when(level == 1)
    def _():
        stage(lax.div(q1, 4) * 128 + lax.rem(q1, 4) * 8, 8)
        compact(32)

    @pl.when(level == 0)
    def _():
        stage(lax.div(q0, 2) * 128 + lax.rem(q0, 2) * 8, 8)
        compact(16)

    @pl.when(level == 3)
    def _():
        for i in (2, 3, 4, 0, 1, 5):
            loads[i].start()

    pl.semaphore_wait(barrier, 45)

    def rows_of(lev, m):
        if lev == 4:
            return (inv_h, op_h)[m].at[0, pl.ds(384, 128)], (gpz, gkz)[m]
        if lev == 3:
            return (inv_h, op_h)[m].at[0, pl.ds(row3, 24)], (gp, gk)[m].at[vb, ub]
        first, count = ((m, 1), (2 + m, 1), (4 + 4 * m, 4))[lev]
        return sg.at[pl.ds(0, count)], gs.at[vb, ub, pl.ds(first, count)]

    def line(lev, m, d):
        source, slot = rows_of(lev, m)
        return pltpu.make_async_remote_copy(
            src_ref=source, dst_ref=slot, send_sem=(zz_sem if lev == 4 else z_sem).at[d], recv_sem=zr_sem.at[lev, m],
            device_id=(lax.rem(z + d, 8), g - c + bb), device_id_type=MESH,
        )

    def to_sibling(lev, m):
        source, slot = rows_of(lev, m)
        return pltpu.make_async_remote_copy(
            src_ref=source, dst_ref=slot, send_sem=(zz_sem if lev == 4 else z_sem).at[0], recv_sem=zr_sem.at[lev, m],
            device_id=sib, device_id_type=MESH,
        )

    def stays(lev, m):
        source, slot = rows_of(lev, m)
        return pltpu.make_async_copy(source, slot, own_sem.at[lev, m])

    def to_line(lev, m):
        @pl.when((level == min(lev, 3)) & (c == m))
        def _():
            for d in (4, 3, 5, 2, 6, 1, 7):
                line(lev, m, d).start()

        @pl.when((level == min(lev, 3)) & (c == m) & (bb != m))
        def _():
            to_sibling(lev, m).start()

        @pl.when((level == min(lev, 3)) & (c == m) & (bb == m))
        def _():
            stays(lev, m).start()

    for lev in range(3):
        to_line(lev, 0)
        to_line(lev, 1)
    to_line(3, 0)

    def send(k, i, src, to):
        return pltpu.make_async_remote_copy(
            src_ref=src, dst_ref=src, send_sem=ring_s.at[k, i], recv_sem=ring_r.at[k, i],
            device_id=to, device_id_type=MESH,
        )

    def steps_of(k, b):
        return {
            "a": [send(k, i, b.at[v, u], plane(v, to)) for i, to in enumerate((u_up, u_down, u_far))],
            "c": [send(k, 3, b.at[v], plane(v_up, u)), send(k, 4, b.at[v], plane(v_down, u))],
            "d": [
                send(k, 5, b.at[v_down, pl.ds(0, 2)], plane(v_up, u)),
                send(k, 6, b.at[v_up, pl.ds(2, 2)], plane(v_down, u)),
            ],
        }

    kinds = [steps_of(0, gs), steps_of(1, gp), steps_of(2, gk)]

    def go(k, *names):
        for name in names:
            for copy in kinds[k][name]:
                copy.start()

    def arrived(k, *names):
        for name in names:
            for copy in kinds[k][name]:
                copy.wait_recv()

    def landing(lev, m):
        if lev == 4:
            slot = (gpz, gkz)[m]
        elif lev == 3:
            slot = (gp, gk)[m].at[v, u]
        else:
            first, count = ((m, 1), (2 + m, 1), (4 + 4 * m, 4))[lev]
            slot = gs.at[v, u, pl.ds(first, count)]
        return pltpu.make_async_remote_copy(
            src_ref=slot, dst_ref=slot, send_sem=z_sem.at[0], recv_sem=zr_sem.at[lev, m],
            device_id=sib, device_id_type=MESH,
        )

    def from_line(k):
        for lev, m in (((0, 0), (0, 1), (1, 0), (1, 1), (2, 0), (2, 1)), ((3, 0),), ((3, 1),), ((4, 0),), ((4, 1),))[k]:

            @pl.when((z != 4 * c + min(lev, 3)) | (c != m))
            def _(lev=lev, m=m):
                landing(lev, m).wait_recv()

            @pl.when((z == 4 * c + min(lev, 3)) & (c == m))
            def _(lev=lev, m=m):
                stays(lev, m).wait()

    load_bucket.wait()
    load_len.wait()
    load_attach.wait()
    bucket = bucket_ref[...]
    own_level = jnp.bitwise_and(bucket, 3)
    counts = jnp.left_shift(jnp.full((1, FIB), 16, jnp.int32), own_level)
    marks = (lax.broadcasted_iota(jnp.int32, (16, FIB), 0) == bucket).astype(F32)
    before = lax.broadcasted_iota(jnp.int32, (FIB, FIB), 0) < lax.broadcasted_iota(jnp.int32, (FIB, FIB), 1)
    ranks = dot_nn(marks.astype(BF16), before.astype(F32).astype(BF16))
    rank = jnp.sum(ranks * marks, axis=0, keepdims=True)
    upper = jnp.right_shift(bucket, 2)
    other = upper + c - 2 * c * upper
    column = (own_level * 256 + other * 128).astype(F32) + rank
    for i in range(8):
        place = (lax.broadcasted_iota(jnp.int32, (128, FIB), 0) + 128 * i).astype(F32)
        mt[128 * i : 128 * (i + 1), :] = (place == column).astype(F32).astype(BF16)

    lengths = len_ref[...]
    attach = attach_ref[...]
    row = lax.broadcasted_iota(jnp.int32, (16, FIB), 0)
    which = jnp.bitwise_and(row, 7)
    extra = jnp.where(which == 0, 0.3 / lengths, jnp.where(which == 1, lengths / counts.astype(F32), 0.0))
    extra = jnp.where(which == 2, attach.astype(F32), extra)
    hi = extra.astype(BF16).astype(F32)
    xhl[1792:1808, :] = jnp.where(row < 8, hi, extra - hi).astype(BF16)

    load_rhs.wait()
    load_off.wait()
    for cc in range(7):
        hi, lo = split2(rhs[cc] if cc < 4 else off[cc - 4])
        xhl[256 * cc : 256 * cc + 128, :] = hi
        xhl[256 * cc + 128 : 256 * cc + 256, :] = lo

    fibers, leaving = (f0, f1, f2, f3), (t0, t1, t2, t3)
    xs, backs = (x0, x1, x2, x3), (b0, b1, b2, b3)

    def cross_over(lev):
        return pltpu.make_async_remote_copy(
            src_ref=leaving[lev], dst_ref=fibers[lev].at[c], send_sem=fib_s.at[lev], recv_sem=fib_r.at[lev],
            device_id=sib, device_id_type=MESH,
        )

    def come_back(lev):
        return pltpu.make_async_remote_copy(
            src_ref=xs[lev].at[1 - c], dst_ref=backs[lev], send_sem=back_s.at[lev], recv_sem=back_r.at[lev],
            device_id=sib, device_id_type=MESH,
        )

    def regroup(lev):
        n = NODES[lev]
        slots = mt[256 * lev : 256 * lev + 256, :]
        if lev == 3:
            left = xhl[...]
        else:
            left = jnp.concatenate([xhl[128 * i : 128 * i + n, :] for i in range(14)] + [xhl[1792:1808, :]], axis=0)
        moved = dot_nt(left, slots)
        for cc in range(7):
            value = moved[2 * n * cc : 2 * n * cc + n] + moved[2 * n * cc + n : 2 * n * cc + 2 * n]
            fibers[lev][c, n * cc : n * cc + n, :] = value[:, :128]
            leaving[lev][n * cc : n * cc + n, :] = value[:, 128:]
        value = moved[14 * n : 14 * n + 8] + moved[14 * n + 8 : 14 * n + 16]
        fibers[lev][c, 7 * n : 7 * n + 8, :] = value[:, :128]
        leaving[lev][7 * n : 7 * n + 8, :] = value[:, 128:]
        cross_over(lev).start()

    to_line(3, 1)
    from_line(0)
    go(0, "a")
    from_line(1)
    go(1, "a")
    to_line(4, 0)
    regroup(2)
    regroup(1)
    regroup(0)
    arrived(0, "a")
    go(0, "c")
    from_line(2)
    go(2, "a")
    arrived(1, "a")
    go(1, "c")
    to_line(4, 1)
    regroup(3)
    arrived(2, "a")
    go(2, "c")

    load_mob.wait()
    wide = jnp.concatenate([mob_ref[...], jnp.zeros((36, 64), F32)], axis=1)
    mob[c, 0:36, :] = jnp.where(c == 0, wide, pltpu.roll(wide, 64, 1))
    send_mob = pltpu.make_async_remote_copy(
        src_ref=mob.at[c], dst_ref=mob.at[c], send_sem=mob_s, recv_sem=mob_r, device_id=sib, device_id_type=MESH
    )
    send_mob.start()
    arrived(0, "c")
    go(0, "d")

    chip = jnp.right_shift(attach, 7)
    place = lax.broadcasted_iota(jnp.int32, (128, FIB), 0)
    fhot[...] = (place == jnp.bitwise_and(attach, 127)).astype(F32).astype(BF16)
    for lev in range(4):
        n = NODES[lev]
        cross_over(lev).wait_recv()
        for o in range(2):
            asl[0:1, 256 * lev + 128 * o : 256 * lev + 128 * o + 128] = fibers[lev][o, 7 * n + 2 : 7 * n + 3, :]
    slot_chip = jnp.floor(asl[0:1, :] * (1 / 128))
    slot_place = asl[0:1, :] - 128 * slot_chip
    place = lax.broadcasted_iota(jnp.int32, (128, 1024), 0).astype(F32)
    shot[...] = (place == slot_place).astype(F32).astype(BF16)
    arrived(1, "c")
    go(1, "d")

    def split_into(ref, i, matrix):
        hi, lo = split2(matrix)
        m = matrix.shape[0]
        ref[i, 0:m, :] = hi
        ref[i, m : 2 * m, :] = lo

    mats = (m0, m1, m2, m3)

    def times(lev, i, w):
        if lev == 0:
            w = jnp.concatenate([w, jnp.zeros_like(w)], axis=0)
        return product(mats[lev].at[i], w)

    def both(ref, rows):
        return jnp.concatenate([ref[0, 0:rows, :], ref[1, 0:rows, :]], axis=1)

    def keep(lev, value):
        xs[lev][0] = value[:, :128]
        xs[lev][1] = value[:, 128:]

    def begin(lev):
        keep(lev, times(lev, 0, both(fibers[lev], 4 * NODES[lev])))

    def paired(lev, i, w):
        hi, lo = split2(w)
        right = jnp.concatenate([hi, lo], axis=1)
        if lev == 0:
            right = jnp.concatenate([right, jnp.zeros_like(right)], axis=0)
        r = dot_nn(mats[lev][i], right)
        m = r.shape[0] // 2
        return r[:m, :128] + (r[:m, 128:] + r[m:, :128])

    def sweep(lev):
        n = NODES[lev]
        held, fib = xs[lev], fibers[lev]
        for o in range(2):
            now = held[o]
            pulled = paired(lev, 1, now)
            f = fib[o, 7 * n : 7 * n + 1, :]
            a = [fib[o, n * (4 + i) : n * (5 + i), :] for i in range(3)]
            w = [now[n * i : n * i + n, :] for i in range(4)]
            along = 0.15 * (a[0] * w[0] + a[1] * w[1] + a[2] * w[2])
            across = along + 0.15 * w[3]
            left = [
                fib[o, n * i : n * i + n, :] - f * pulled[n * i : n * i + n] - (a[i] * across if i < 3 else along)
                for i in range(4)
            ]
            held[o] = paired(lev, 0, jnp.concatenate(left, axis=0))

    def wrench_of(lev):
        n = NODES[lev]
        for o in range(2):
            a = [fibers[lev][o, n * (4 + i) : n * (5 + i), :] for i in range(3)]
            w = [xs[lev][o, n * i : n * i + n, :] for i in range(3)]
            weight = fibers[lev][o, 7 * n + 1 : 7 * n + 2, :]
            parts = w + [a[1] * w[2] - a[2] * w[1], a[2] * w[0] - a[0] * w[2], a[0] * w[1] - a[1] * w[0]]
            for i, part in enumerate(parts):
                wr[i : i + 1, 256 * lev + 128 * o : 256 * lev + 128 * o + 128] = (
                    jnp.sum(part, axis=0, keepdims=True) * weight
                )

    wr[...] = jnp.zeros_like(wr)
    arrived(0, "d")
    for m in range(2):
        split_into(m0, m, gs[0:2, :, m].reshape(64, 128))
        split_into(m1, m, gs[:, :, 2 + m].reshape(128, 128))
        left, right = [gs[:, :, 4 + 4 * m + 2 * h : 6 + 4 * m + 2 * h].reshape(256, 128) for h in range(2)]
        split_into(m2, m, jnp.concatenate([left, right], axis=1))
    for lev in range(3):
        begin(lev)

    def small_sweeps(i, n):
        for lev in range(3):
            sweep(lev)
        return n

    lax.fori_loop(0, 1, small_sweeps, 0)
    arrived(2, "c")
    go(2, "d")
    lax.fori_loop(1, ITERS, small_sweeps, 0)
    for lev in range(3):
        come_back(lev).start()
        wrench_of(lev)

    arrived(1, "d")
    from_line(3)
    split_into(m3, 0, jnp.concatenate([gp[...].reshape(384, 512), gpz[...]], axis=0))
    begin(3)
    arrived(2, "d")
    from_line(4)
    split_into(m3, 1, jnp.concatenate([gk[...].reshape(384, 512), gkz[...]], axis=0))

    def large_sweeps(i, n):
        sweep(3)
        return n

    for i in range(ITERS):
        large_sweeps(i, 0)
    come_back(3).start()
    wrench_of(3)
    hi = wr[...].astype(BF16).astype(F32)
    terms = jnp.concatenate([hi, wr[...] - hi], axis=0)
    left = jnp.concatenate([jnp.where(slot_chip == q, terms, 0.0).astype(BF16) for q in range(16)], axis=0)
    table = dot_nt(left, shot[...])
    for q in range(16):
        tab[q] = table[16 * q : 16 * q + 8] + table[16 * q + 8 : 16 * q + 16]
    got[g] = tab[lax.div(g, 2)]
    for d in range(1, 32):
        to = lax.rem(g + d, 32)
        pltpu.make_async_remote_copy(
            src_ref=tab.at[lax.div(to, 2)], dst_ref=got.at[g], send_sem=t_s, recv_sem=t_r,
            device_id=(z, to), device_id_type=MESH,
        ).start()

    for lev in (2, 1, 0, 3):
        come_back(lev).wait_recv()
    for lev in (3, 2, 1, 0):
        n = NODES[lev]
        hi, lo = split2(jnp.concatenate([xs[lev][c], backs[lev][...]], axis=1))
        moved = dot_nn(jnp.concatenate([hi, lo], axis=0), mt[256 * lev : 256 * lev + 256, :])
        for cc in range(4):
            value = moved[n * cc : n * cc + n] + moved[4 * n + n * cc : 4 * n + n * cc + n]
            if lev == 3:
                sol[cc] = value
            else:
                sol[cc, 0:n, :] += value
    save = pltpu.make_async_copy(sol, sol_h, sol_sem)
    save.start()

    send_mob.wait()
    for lev in range(4):
        cross_over(lev).wait_send()
        come_back(lev).wait_send()
    for steps in kinds:
        for copies in steps.values():
            for copy in copies:
                copy.wait_send()
    for lev in range(5):
        for m in range(2):

            @pl.when((level == min(lev, 3)) & (c == m))
            def _(lev=lev, m=m):
                for d in range(1, 8):
                    line(lev, m, d).wait_send()

            @pl.when((level == min(lev, 3)) & (c == m) & (bb != m))
            def _(lev=lev, m=m):
                to_sibling(lev, m).wait_send()

    many = got.at[pl.ds(0, 31)]
    tables = pltpu.make_async_remote_copy(
        src_ref=many, dst_ref=many, send_sem=t_s, recv_sem=t_r, device_id=sib, device_id_type=MESH
    )
    tables.wait_send()
    tables.wait_recv()
    total = got[0]
    for i in range(1, 32):
        total = total + got[i]
    pair = mob[0, 0:36, :] + mob[1, 0:36, :]
    mine = lax.div(g, 2)
    rows = []
    for k in range(6):
        one = pair[6 * k : 6 * k + 1] * total[0:1]
        for j in range(1, 6):
            one = one + pair[6 * k + j : 6 * k + j + 1] * total[j : j + 1]
        rows.append(one)
    mot[mine] = jnp.concatenate(rows + [jnp.zeros((2, 128), F32)], axis=0)
    for d in range(1, 16):
        pltpu.make_async_remote_copy(
            src_ref=mot.at[mine], dst_ref=mot.at[mine], send_sem=mo_s, recv_sem=mo_r,
            device_id=(z, lax.rem(mine + d, 16) * 2 + c), device_id_type=MESH,
        ).start()
    most = mot.at[pl.ds(0, 15)]
    motions_come = pltpu.make_async_remote_copy(
        src_ref=most, dst_ref=most, send_sem=mo_s, recv_sem=mo_r, device_id=sib, device_id_type=MESH
    )
    motions_come.wait_send()
    motions_come.wait_recv()
    hi, lo = split2(mot[...].reshape(128, 128))
    parts = dot_nn(jnp.concatenate([hi, lo], axis=0), fhot[...])
    moving = jnp.zeros((8, FIB), F32)
    for q in range(16):
        moving = jnp.where(chip == q, parts[8 * q : 8 * q + 8] + parts[128 + 8 * q : 136 + 8 * q], moving)
    moving_ref[...] = moving
    save.wait()


def add_motion(sol_ref, off_ref, moving_ref, bucket_ref, out_ref):
    counts = jnp.left_shift(jnp.full((1, FIB), 16, jnp.int32), jnp.bitwise_and(bucket_ref[...], 3))
    live = lax.broadcasted_iota(jnp.int32, (64, FIB), 0) + 64 * pl.program_id(0) < counts
    moving = moving_ref[...]
    a = [off_ref[i] for i in range(3)]
    for i in range(3):
        j, k = (i + 1) % 3, (i + 2) % 3
        turn = moving[3 + j : 4 + j] * a[k] - moving[3 + k : 4 + k] * a[j]
        out_ref[i] = sol_ref[i] + jnp.where(live, moving[i : i + 1] + turn, 0.0)
    out_ref[3] = sol_ref[3]


def body(rhs, offsets, lengths, bucket, attach, operator, inverse, mobility):
    hbm, vmem = pl.BlockSpec(memory_space=pltpu.HBM), pl.BlockSpec(memory_space=pltpu.VMEM)
    dma = pltpu.SemaphoreType.DMA
    scratch = [
        pltpu.VMEM((1, FIB), F32), pltpu.VMEM((1, FIB), jnp.int32), pltpu.VMEM((1, FIB), jnp.int32),
        pltpu.VMEM((36, CEN), F32),
        pltpu.VMEM((4, 128, FIB), F32), pltpu.VMEM((3, 128, FIB), F32),
        pltpu.VMEM((4, 4, 12, 8, 128), F32),
        pltpu.VMEM((4, 4, 24, 512), F32), pltpu.VMEM((4, 4, 24, 512), F32),
        pltpu.VMEM((128, 512), F32), pltpu.VMEM((128, 512), F32),
        pltpu.VMEM((16, 512), F32), pltpu.VMEM((4, 8, 128), F32),
        pltpu.VMEM((2, 1024, 512), BF16), pltpu.VMEM((2, 512, 256), BF16),
        pltpu.VMEM((2, 256, 128), BF16), pltpu.VMEM((2, 128, 128), BF16),
        pltpu.VMEM((1024, FIB), BF16), pltpu.VMEM((7 * 256 + 16, FIB), BF16), pltpu.VMEM((128, FIB), BF16),
        pltpu.VMEM((128, 1024), BF16), pltpu.VMEM((4, 128, FIB), F32),
        *[pltpu.VMEM((2, 7 * n + 8, 128), F32) for n in NODES[::-1]],
        *[pltpu.VMEM((7 * n + 8, 128), F32) for n in NODES[::-1]],
        *[pltpu.VMEM((2, 4 * n, 128), F32) for n in NODES[::-1]],
        *[pltpu.VMEM((4 * n, 128), F32) for n in NODES[::-1]],
        pltpu.VMEM((8, 1024), F32), pltpu.VMEM((8, 1024), F32),
        pltpu.VMEM((16, 8, 128), F32), pltpu.VMEM((32, 8, 128), F32), pltpu.VMEM((16, 8, 128), F32),
        pltpu.VMEM((2, 40, 128), F32),
        dma, dma((6,)), dma, dma((5, 2)), dma((8,)), dma((8,)), dma((5, 2)),
        dma((3, 7)), dma((3, 7)), dma((4,)), dma((4,)), dma((4,)), dma((4,)),
        dma, dma, dma, dma, dma, dma,
    ]
    bucket = bucket.reshape(1, FIB)
    solved, moving = pl.pallas_call(
        kernel,
        out_shape=(jax.ShapeDtypeStruct((4, 128, FIB), F32), jax.ShapeDtypeStruct((8, FIB), F32)),
        in_specs=[hbm] * 8,
        out_specs=(hbm, vmem),
        scratch_shapes=scratch,
        compiler_params=pltpu.CompilerParams(
            collective_id=0, has_side_effects=True, vmem_limit_bytes=60 * 2**20
        ),
    )(
        rhs, offsets, lengths.reshape(1, FIB), bucket, attach.reshape(1, FIB), operator, inverse, mobility,
    )

    def nodes(rows):
        return pl.BlockSpec((rows, 64, FIB), lambda i: (0, i, 0))

    return pl.pallas_call(
        add_motion,
        grid=(2,),
        out_shape=jax.ShapeDtypeStruct((4, 128, FIB), F32),
        in_specs=[
            nodes(4), nodes(3), pl.BlockSpec((8, FIB), lambda i: (0, 0)), pl.BlockSpec((1, FIB), lambda i: (0, 0)),
        ],
        out_specs=nodes(4),
        compiler_params=pltpu.CompilerParams(vmem_limit_bytes=60 * 2**20),
    )(solved, offsets, moving, bucket)


def solution(mesh):
    both = ("gx", "gy")
    in_specs = (
        P(None, None, both), P(None, None, both), P(both), P(both, None), P(both),
        P("gx", None, None), P("gx", None, None), P(None, both),
    )
    return jax.shard_map(body, mesh=mesh, in_specs=in_specs, out_specs=P(None, None, both), check_vma=False)
```

```python
import jax
import jax.numpy as jnp
from jax import lax
from jax.experimental import pallas as pl
from jax.experimental.pallas import tpu as pltpu
from jax.sharding import PartitionSpec as P

ITERS = 4
FIB = 512
CEN = 64
MESH = pl.DeviceIdType.MESH
F32, BF16 = jnp.float32, jnp.bfloat16
NODES = (16, 32, 64, 128)


def dot_nn(a, b):
    return lax.dot_general(a, b, (((1,), (0,)), ((), ())), preferred_element_type=F32)


def dot_nt(a, b):
    return lax.dot_general(a, b, (((1,), (1,)), ((), ())), preferred_element_type=F32)


def split2(x):
    hi = x.astype(BF16)
    return hi, (x - hi.astype(F32)).astype(BF16)


def product(matrix, x):
    hi, lo = split2(x)
    m = matrix.shape[0] // 2
    first = dot_nn(matrix[...], hi)
    return first[:m] + (first[m:] + dot_nn(matrix[0:m, :], lo))


def kernel(
    rhs_h, off_h, len_h, bucket_h, attach_h, op_h, inv_h, mob_h, sol_h, moving_ref,
    len_ref, bucket_ref, attach_ref, mob_ref, rhs, off, gs, gp, gk, gpz, gkz, st, sg, whole, prow, pkr, xz,
    m3, m2, m1, m0, mt, xhl, fhot, shot, sol,
    f3, f2, f1, f0, t3, t2, t1, t0, x3, x2, x1, x0, b3, b2, b1, b0, wr, asl,
    tab, got, mot, mob,
    sol_sem, in_sem, st_sem, pk_sem, own_sem, z_sem, zz_sem, zr_sem,
    ring_s, ring_r, fib_s, fib_r, back_s, back_r, t_s, t_r, mo_s, mo_r, mob_s, mob_r,
):
    z = lax.axis_index("gx")
    g = lax.axis_index("gy")
    x, y, c = lax.div(g, 8), lax.rem(lax.div(g, 2), 4), lax.rem(g, 2)
    u, v = x + c * (y - x), y + c * (x - y)
    level, bb = lax.rem(z, 4), lax.div(z, 4)
    ub, vb = x + bb * (y - x), y + bb * (x - y)
    rb = vb * 4 + ub
    away = c + bb - 2 * c * bb

    def plane(vv, uu):
        xx, yy = uu + c * (vv - uu), vv + c * (uu - vv)
        return (z, (xx * 4 + yy) * 2 + c)

    u_up, u_down = lax.rem(u + 1, 4), lax.rem(u + 3, 4)
    v_up, v_down = lax.rem(v + 1, 4), lax.rem(v + 3, 4)
    u_far = lax.rem(u + 2, 4)
    sib = (z, g + 1 - 2 * c)
    barrier = pltpu.get_barrier_semaphore()
    for d in range(1, 8):
        zz = lax.rem(z + d, 8)
        pl.semaphore_signal(barrier, inc=1, device_id=(zz, g), device_id_type=MESH)
        pl.semaphore_signal(barrier, inc=1, device_id=(zz, g + 1 - 2 * c), device_id_type=MESH)
    for d in range(1, 32):
        pl.semaphore_signal(barrier, inc=1, device_id=(z, lax.rem(g + d, 32)), device_id_type=MESH)

    load_rhs, load_off, load_bucket, load_len, load_attach, load_mob = loads = [
        pltpu.make_async_copy(source, place, in_sem.at[i])
        for i, (source, place) in enumerate((
            (rhs_h, rhs), (off_h, off), (bucket_h, bucket_ref),
            (len_h, len_ref), (attach_h, attach_ref), (mob_h, mob_ref),
        ))
    ]

    def stage(row, count):
        row = pl.multiple_of(row, 8)

        @pl.when(c == 0)
        def _():
            pltpu.make_async_copy(inv_h.at[0, pl.ds(row, count)], st.at[pl.ds(0, count)], st_sem).start()

        @pl.when(c == 1)
        def _():
            pltpu.make_async_copy(op_h.at[0, pl.ds(row, count)], st.at[pl.ds(0, count)], st_sem).start()

        for i in (2, 3, 4, 0, 1, 5):
            loads[i].start()
        pltpu.make_async_copy(inv_h.at[0, pl.ds(row, count)], st.at[pl.ds(0, count)], st_sem).wait()

    def lanes_of(rows):
        return lax.broadcasted_iota(jnp.int32, (rows, 128), 1)

    q1, q0 = rb, lax.rem(rb, 8)
    row3 = pl.multiple_of(rb * 24, 8)

    @pl.when(level == 2)
    def _():
        stage(lax.div(rb, 4) * 128 + lax.rem(rb, 4) * 16, 16)
        for h in range(2):
            left = st[:, 256 * h : 256 * h + 128]
            right = st[:, 256 * h + 128 : 256 * h + 256]
            part = jnp.where(lanes_of(16) < 64, left, pltpu.roll(right, 64, 1))
            sg[2 * h] = part[0:8]
            sg[2 * h + 1] = part[8:16]

    def compact(width):
        lane = lanes_of(8)
        total = jnp.zeros((8, 128), F32)
        for i in range(4):
            part = st[0:8, 128 * i : 128 * i + 128]
            part = pltpu.roll(part, width * i, 1) if i else part
            total = jnp.where((lane >= width * i) & (lane < width * i + width), part, total)
        sg[0] = total

    @pl.when(level == 1)
    def _():
        stage(lax.div(q1, 4) * 128 + lax.rem(q1, 4) * 8, 8)
        compact(32)

    @pl.when(level == 0)
    def _():
        stage(lax.div(q0, 2) * 128 + lax.rem(q0, 2) * 8, 8)
        compact(16)

    product_loads = [
        pltpu.make_async_copy(source, place, pk_sem.at[i])
        for i, (source, place) in enumerate((
            (inv_h.at[0, pl.ds(row3, 32)], prow.at[pl.ds(0, 32)]),
            (inv_h.at[0, pl.ds(384, 128)], prow.at[pl.ds(32, 128)]),
            (op_h.at[0], whole),
        ))
    ]

    @pl.when(level == 3)
    def _():
        for i in (2, 3, 4, 0, 1, 5):
            loads[i].start()

    @pl.when((level == 3) & (c == 1))
    def _():
        for copy in product_loads:
            copy.start()

    @pl.when((level == 3) & (c == 1))
    def _():
        for copy in product_loads:
            copy.wait()
        hi, lo = split2(prow[...])
        over, under = split2(whole[...])
        first = dot_nn(jnp.concatenate([hi, lo], axis=0), over)
        pkr[...] = first[:160] + (first[160:] + dot_nn(hi, under))

    pl.semaphore_wait(barrier, 45)

    def rows_of(lev, m):
        if lev == 4:
            return (pkr.at[pl.ds(32, 128)] if m else inv_h.at[0, pl.ds(384, 128)]), (gpz, gkz)[m]
        if lev == 3:
            return (pkr.at[pl.ds(0, 24)] if m else inv_h.at[0, pl.ds(row3, 24)]), (gp, gk)[m].at[vb, ub]
        first, count = ((m, 1), (2 + m, 1), (4 + 4 * m, 4))[lev]
        return sg.at[pl.ds(0, count)], gs.at[vb, ub, pl.ds(first, count)]

    def line(lev, m, d):
        source, slot = rows_of(lev, m)
        return pltpu.make_async_remote_copy(
            src_ref=source, dst_ref=slot, send_sem=(zz_sem if lev == 4 else z_sem).at[d], recv_sem=zr_sem.at[lev, m],
            device_id=(lax.rem(z + d, 8), g - c + bb), device_id_type=MESH,
        )

    def to_sibling(lev, m):
        source, slot = rows_of(lev, m)
        return pltpu.make_async_remote_copy(
            src_ref=source, dst_ref=slot, send_sem=(zz_sem if lev == 4 else z_sem).at[0], recv_sem=zr_sem.at[lev, m],
            device_id=sib, device_id_type=MESH,
        )

    def stays(lev, m):
        source, slot = rows_of(lev, m)
        return pltpu.make_async_copy(source, slot, own_sem.at[lev, m])

    def to_line(lev, m):
        @pl.when((level == min(lev, 3)) & (c == m))
        def _():
            for d in (4, 3, 5, 2, 6, 1, 7):
                line(lev, m, d).start()

        @pl.when((level == min(lev, 3)) & (c == m) & (bb != m))
        def _():
            to_sibling(lev, m).start()

        @pl.when((level == min(lev, 3)) & (c == m) & (bb == m))
        def _():
            stays(lev, m).start()

    for lev in range(3):
        to_line(lev, 0)
        to_line(lev, 1)
    to_line(3, 0)

    def send(k, i, src, to):
        return pltpu.make_async_remote_copy(
            src_ref=src, dst_ref=src, send_sem=ring_s.at[k, i], recv_sem=ring_r.at[k, i],
            device_id=to, device_id_type=MESH,
        )

    def steps_of(k, b):
        return {
            "a": [send(k, i, b.at[v, u], plane(v, to)) for i, to in enumerate((u_up, u_down, u_far))],
            "c": [send(k, 3, b.at[v], plane(v_up, u)), send(k, 4, b.at[v], plane(v_down, u))],
            "d": [
                send(k, 5, b.at[v_down, pl.ds(0, 2)], plane(v_up, u)),
                send(k, 6, b.at[v_up, pl.ds(2, 2)], plane(v_down, u)),
            ],
        }

    kinds = [steps_of(0, gs), steps_of(1, gp), steps_of(2, gk)]

    def go(k, *names):
        for name in names:
            for copy in kinds[k][name]:
                copy.start()

    def arrived(k, *names):
        for name in names:
            for copy in kinds[k][name]:
                copy.wait_recv()

    def landing(lev, m):
        if lev == 4:
            slot = (gpz, gkz)[m]
        elif lev == 3:
            slot = (gp, gk)[m].at[v, u]
        else:
            first, count = ((m, 1), (2 + m, 1), (4 + 4 * m, 4))[lev]
            slot = gs.at[v, u, pl.ds(first, count)]
        return pltpu.make_async_remote_copy(
            src_ref=slot, dst_ref=slot, send_sem=z_sem.at[0], recv_sem=zr_sem.at[lev, m],
            device_id=sib, device_id_type=MESH,
        )

    def from_line(k):
        for lev, m in (((0, 0), (0, 1), (1, 0), (1, 1), (2, 0), (2, 1)), ((3, 0),), ((3, 1),), ((4, 0),), ((4, 1),))[k]:

            @pl.when((z != 4 * c + min(lev, 3)) | (c != m))
            def _(lev=lev, m=m):
                landing(lev, m).wait_recv()

            @pl.when((z == 4 * c + min(lev, 3)) & (c == m))
            def _(lev=lev, m=m):
                stays(lev, m).wait()

    load_bucket.wait()
    load_len.wait()
    load_attach.wait()
    bucket = bucket_ref[...]
    own_level = jnp.bitwise_and(bucket, 3)
    counts = jnp.left_shift(jnp.full((1, FIB), 16, jnp.int32), own_level)
    marks = (lax.broadcasted_iota(jnp.int32, (16, FIB), 0) == bucket).astype(F32)
    before = lax.broadcasted_iota(jnp.int32, (FIB, FIB), 0) < lax.broadcasted_iota(jnp.int32, (FIB, FIB), 1)
    ranks = dot_nn(marks.astype(BF16), before.astype(F32).astype(BF16))
    rank = jnp.sum(ranks * marks, axis=0, keepdims=True)
    upper = jnp.right_shift(bucket, 2)
    other = upper + c - 2 * c * upper
    column = (own_level * 256 + other * 128).astype(F32) + rank
    for i in range(8):
        place = (lax.broadcasted_iota(jnp.int32, (128, FIB), 0) + 128 * i).astype(F32)
        mt[128 * i : 128 * (i + 1), :] = (place == column).astype(F32).astype(BF16)

    lengths = len_ref[...]
    attach = attach_ref[...]
    row = lax.broadcasted_iota(jnp.int32, (16, FIB), 0)
    which = jnp.bitwise_and(row, 7)
    extra = jnp.where(which == 0, 0.3 / lengths, jnp.where(which == 1, lengths / counts.astype(F32), 0.0))
    extra = jnp.where(which == 2, attach.astype(F32), extra)
    hi = extra.astype(BF16).astype(F32)
    xhl[1792:1808, :] = jnp.where(row < 8, hi, extra - hi).astype(BF16)

    to_line(3, 1)
    load_rhs.wait()
    load_off.wait()
    for cc in range(7):
        hi, lo = split2(rhs[cc] if cc < 4 else off[cc - 4])
        xhl[256 * cc : 256 * cc + 128, :] = hi
        xhl[256 * cc + 128 : 256 * cc + 256, :] = lo

    fibers, leaving = (f0, f1, f2, f3), (t0, t1, t2, t3)
    xs, backs = (x0, x1, x2, x3), (b0, b1, b2, b3)

    def cross_over(lev):
        return pltpu.make_async_remote_copy(
            src_ref=leaving[lev], dst_ref=fibers[lev].at[c], send_sem=fib_s.at[lev], recv_sem=fib_r.at[lev],
            device_id=sib, device_id_type=MESH,
        )

    def come_back(lev):
        return pltpu.make_async_remote_copy(
            src_ref=xs[lev].at[1 - c], dst_ref=backs[lev], send_sem=back_s.at[lev], recv_sem=back_r.at[lev],
            device_id=sib, device_id_type=MESH,
        )

    def regroup(lev):
        n = NODES[lev]
        slots = mt[256 * lev : 256 * lev + 256, :]
        if lev == 3:
            left = xhl[...]
        else:
            left = jnp.concatenate([xhl[128 * i : 128 * i + n, :] for i in range(14)] + [xhl[1792:1808, :]], axis=0)
        moved = dot_nt(left, slots)
        for cc in range(7):
            value = moved[2 * n * cc : 2 * n * cc + n] + moved[2 * n * cc + n : 2 * n * cc + 2 * n]
            fibers[lev][c, n * cc : n * cc + n, :] = value[:, :128]
            leaving[lev][n * cc : n * cc + n, :] = value[:, 128:]
        value = moved[14 * n : 14 * n + 8] + moved[14 * n + 8 : 14 * n + 16]
        fibers[lev][c, 7 * n : 7 * n + 8, :] = value[:, :128]
        leaving[lev][7 * n : 7 * n + 8, :] = value[:, 128:]
        cross_over(lev).start()

    from_line(0)
    go(0, "a")
    from_line(1)
    go(1, "a")
    to_line(4, 0)
    regroup(2)
    regroup(1)
    regroup(0)
    arrived(0, "a")
    go(0, "c")
    from_line(2)
    go(2, "a")
    arrived(1, "a")
    go(1, "c")
    to_line(4, 1)
    arrived(2, "a")
    go(2, "c")
    regroup(3)

    load_mob.wait()
    wide = jnp.concatenate([mob_ref[...], jnp.zeros((36, 64), F32)], axis=1)
    mob[c, 0:36, :] = jnp.where(c == 0, wide, pltpu.roll(wide, 64, 1))
    send_mob = pltpu.make_async_remote_copy(
        src_ref=mob.at[c], dst_ref=mob.at[c], send_sem=mob_s, recv_sem=mob_r, device_id=sib, device_id_type=MESH
    )
    send_mob.start()
    arrived(0, "c")
    go(0, "d")

    chip = jnp.right_shift(attach, 7)
    place = lax.broadcasted_iota(jnp.int32, (128, FIB), 0)
    fhot[...] = (place == jnp.bitwise_and(attach, 127)).astype(F32).astype(BF16)
    for lev in range(4):
        n = NODES[lev]
        cross_over(lev).wait_recv()
        for o in range(2):
            asl[0:1, 256 * lev + 128 * o : 256 * lev + 128 * o + 128] = fibers[lev][o, 7 * n + 2 : 7 * n + 3, :]
    slot_chip = jnp.floor(asl[0:1, :] * (1 / 128))
    slot_place = asl[0:1, :] - 128 * slot_chip
    place = lax.broadcasted_iota(jnp.int32, (128, 1024), 0).astype(F32)
    shot[...] = (place == slot_place).astype(F32).astype(BF16)
    arrived(1, "c")
    go(1, "d")

    def split_into(ref, i, matrix):
        hi, lo = split2(matrix)
        m = matrix.shape[0]
        ref[i, 0:m, :] = hi
        ref[i, m : 2 * m, :] = lo

    mats = (m0, m1, m2, m3)

    def times(lev, i, w):
        if lev == 3:
            return product(m3.at[:, pl.ds(512, 512)], w)
        if lev == 0:
            w = jnp.concatenate([w, jnp.zeros_like(w)], axis=0)
        return product(mats[lev].at[i], w)

    def both(ref, rows):
        return jnp.concatenate([ref[0, 0:rows, :], ref[1, 0:rows, :]], axis=1)

    def keep(lev, value):
        xs[lev][0] = value[:, :128]
        xs[lev][1] = value[:, 128:]

    def begin(lev):
        keep(lev, times(lev, 0, both(fibers[lev], 4 * NODES[lev])))

    def paired(lev, i, w):
        hi, lo = split2(w)
        right = jnp.concatenate([hi, lo], axis=1)
        if lev == 0:
            right = jnp.concatenate([right, jnp.zeros_like(right)], axis=0)
        r = dot_nn(mats[lev][i], right)
        m = r.shape[0] // 2
        return r[:m, :128] + (r[:m, 128:] + r[m:, :128])

    def sweep(lev):
        n = NODES[lev]
        held, fib = xs[lev], fibers[lev]
        for o in range(2):
            now = held[o]
            pulled = paired(lev, 1, now)
            f = fib[o, 7 * n : 7 * n + 1, :]
            a = [fib[o, n * (4 + i) : n * (5 + i), :] for i in range(3)]
            w = [now[n * i : n * i + n, :] for i in range(4)]
            along = 0.15 * (a[0] * w[0] + a[1] * w[1] + a[2] * w[2])
            across = along + 0.15 * w[3]
            left = [
                fib[o, n * i : n * i + n, :] - f * pulled[n * i : n * i + n] - (a[i] * across if i < 3 else along)
                for i in range(4)
            ]
            held[o] = paired(lev, 0, jnp.concatenate(left, axis=0))

    def large_sweep():
        n = NODES[3]
        for o in range(2):
            f = f3[o, 7 * n : 7 * n + 1, :]
            a = [f3[o, n * (4 + i) : n * (5 + i), :] for i in range(3)]
            w = [x3[o, n * i : n * i + n, :] for i in range(4)]
            along = 0.15 * (a[0] * w[0] + a[1] * w[1] + a[2] * w[2])
            across = along + 0.15 * w[3]
            hi, lo = split2(
                jnp.concatenate([f * w[i] for i in range(4)] + [a[i] * across for i in range(3)] + [along], axis=0)
            )
            r = dot_nn(m3[...], jnp.concatenate([hi, lo], axis=1))
            x3[o] = xz[o] - (r[:512, :128] + (r[:512, 128:] + r[512:, :128]))

    def wrench_of(lev):
        n = NODES[lev]
        for o in range(2):
            a = [fibers[lev][o, n * (4 + i) : n * (5 + i), :] for i in range(3)]
            w = [xs[lev][o, n * i : n * i + n, :] for i in range(3)]
            weight = fibers[lev][o, 7 * n + 1 : 7 * n + 2, :]
            parts = w + [a[1] * w[2] - a[2] * w[1], a[2] * w[0] - a[0] * w[2], a[0] * w[1] - a[1] * w[0]]
            for i, part in enumerate(parts):
                wr[i : i + 1, 256 * lev + 128 * o : 256 * lev + 128 * o + 128] = (
                    jnp.sum(part, axis=0, keepdims=True) * weight
                )

    wr[...] = jnp.zeros_like(wr)
    arrived(0, "d")
    for m in range(2):
        split_into(m0, m, gs[0:2, :, m].reshape(64, 128))
        split_into(m1, m, gs[:, :, 2 + m].reshape(128, 128))
        left, right = [gs[:, :, 4 + 4 * m + 2 * h : 6 + 4 * m + 2 * h].reshape(256, 128) for h in range(2)]
        split_into(m2, m, jnp.concatenate([left, right], axis=1))
    for lev in range(3):
        begin(lev)

    def small_sweeps(i, n):
        for lev in range(3):
            sweep(lev)
        return n

    lax.fori_loop(0, 1, small_sweeps, 0)
    arrived(2, "c")
    go(2, "d")
    lax.fori_loop(1, ITERS, small_sweeps, 0)
    for lev in range(3):
        come_back(lev).start()
        wrench_of(lev)

    arrived(1, "d")
    from_line(3)
    hi, lo = split2(jnp.concatenate([gp[...].reshape(384, 512), gpz[...]], axis=0))
    m3[0:512, 512:1024] = hi
    m3[512:1024, 512:1024] = lo
    begin(3)
    xz[...] = x3[...]
    arrived(2, "d")
    from_line(4)
    hi, lo = split2(jnp.concatenate([gk[...].reshape(384, 512), gkz[...]], axis=0))
    m3[0:512, 0:512] = hi
    m3[512:1024, 0:512] = lo
    for i in range(ITERS):
        large_sweep()
    come_back(3).start()
    wrench_of(3)
    hi = wr[...].astype(BF16).astype(F32)
    terms = jnp.concatenate([hi, wr[...] - hi], axis=0)
    left = jnp.concatenate([jnp.where(slot_chip == q, terms, 0.0).astype(BF16) for q in range(16)], axis=0)
    table = dot_nt(left, shot[...])
    for q in range(16):
        tab[q] = table[16 * q : 16 * q + 8] + table[16 * q + 8 : 16 * q + 16]
    got[g] = tab[lax.div(g, 2)]
    for d in range(1, 32):
        to = lax.rem(g + d, 32)
        pltpu.make_async_remote_copy(
            src_ref=tab.at[lax.div(to, 2)], dst_ref=got.at[g], send_sem=t_s, recv_sem=t_r,
            device_id=(z, to), device_id_type=MESH,
        ).start()

    for lev in (2, 1, 0, 3):
        come_back(lev).wait_recv()
    for lev in (3, 2, 1, 0):
        n = NODES[lev]
        hi, lo = split2(jnp.concatenate([xs[lev][c], backs[lev][...]], axis=1))
        moved = dot_nn(jnp.concatenate([hi, lo], axis=0), mt[256 * lev : 256 * lev + 256, :])
        for cc in range(4):
            value = moved[n * cc : n * cc + n] + moved[4 * n + n * cc : 4 * n + n * cc + n]
            if lev == 3:
                sol[cc] = value
            else:
                sol[cc, 0:n, :] += value
    save = pltpu.make_async_copy(sol, sol_h, sol_sem)
    save.start()

    send_mob.wait()
    for lev in range(4):
        cross_over(lev).wait_send()
        come_back(lev).wait_send()
    for steps in kinds:
        for copies in steps.values():
            for copy in copies:
                copy.wait_send()
    for lev in range(5):
        for m in range(2):

            @pl.when((level == min(lev, 3)) & (c == m))
            def _(lev=lev, m=m):
                for d in range(1, 8):
                    line(lev, m, d).wait_send()

            @pl.when((level == min(lev, 3)) & (c == m) & (bb != m))
            def _(lev=lev, m=m):
                to_sibling(lev, m).wait_send()

    many = got.at[pl.ds(0, 31)]
    tables = pltpu.make_async_remote_copy(
        src_ref=many, dst_ref=many, send_sem=t_s, recv_sem=t_r, device_id=sib, device_id_type=MESH
    )
    tables.wait_send()
    tables.wait_recv()
    total = got[0]
    for i in range(1, 32):
        total = total + got[i]
    pair = mob[0, 0:36, :] + mob[1, 0:36, :]
    mine = lax.div(g, 2)
    rows = []
    for k in range(6):
        one = pair[6 * k : 6 * k + 1] * total[0:1]
        for j in range(1, 6):
            one = one + pair[6 * k + j : 6 * k + j + 1] * total[j : j + 1]
        rows.append(one)
    mot[mine] = jnp.concatenate(rows + [jnp.zeros((2, 128), F32)], axis=0)
    for d in range(1, 16):
        pltpu.make_async_remote_copy(
            src_ref=mot.at[mine], dst_ref=mot.at[mine], send_sem=mo_s, recv_sem=mo_r,
            device_id=(z, lax.rem(mine + d, 16) * 2 + c), device_id_type=MESH,
        ).start()
    most = mot.at[pl.ds(0, 15)]
    motions_come = pltpu.make_async_remote_copy(
        src_ref=most, dst_ref=most, send_sem=mo_s, recv_sem=mo_r, device_id=sib, device_id_type=MESH
    )
    motions_come.wait_send()
    motions_come.wait_recv()
    hi, lo = split2(mot[...].reshape(128, 128))
    parts = dot_nn(jnp.concatenate([hi, lo], axis=0), fhot[...])
    moving = jnp.zeros((8, FIB), F32)
    for q in range(16):
        moving = jnp.where(chip == q, parts[8 * q : 8 * q + 8] + parts[128 + 8 * q : 136 + 8 * q], moving)
    moving_ref[...] = moving
    save.wait()


def add_motion(sol_ref, off_ref, moving_ref, bucket_ref, out_ref):
    counts = jnp.left_shift(jnp.full((1, FIB), 16, jnp.int32), jnp.bitwise_and(bucket_ref[...], 3))
    live = lax.broadcasted_iota(jnp.int32, (64, FIB), 0) + 64 * pl.program_id(0) < counts
    moving = moving_ref[...]
    a = [off_ref[i] for i in range(3)]
    for i in range(3):
        j, k = (i + 1) % 3, (i + 2) % 3
        turn = moving[3 + j : 4 + j] * a[k] - moving[3 + k : 4 + k] * a[j]
        out_ref[i] = sol_ref[i] + jnp.where(live, moving[i : i + 1] + turn, 0.0)
    out_ref[3] = sol_ref[3]


def body(rhs, offsets, lengths, bucket, attach, operator, inverse, mobility):
    hbm, vmem = pl.BlockSpec(memory_space=pltpu.HBM), pl.BlockSpec(memory_space=pltpu.VMEM)
    dma = pltpu.SemaphoreType.DMA
    scratch = [
        pltpu.VMEM((1, FIB), F32), pltpu.VMEM((1, FIB), jnp.int32), pltpu.VMEM((1, FIB), jnp.int32),
        pltpu.VMEM((36, CEN), F32),
        pltpu.VMEM((4, 128, FIB), F32), pltpu.VMEM((3, 128, FIB), F32),
        pltpu.VMEM((4, 4, 12, 8, 128), F32),
        pltpu.VMEM((4, 4, 24, 512), F32), pltpu.VMEM((4, 4, 24, 512), F32),
        pltpu.VMEM((128, 512), F32), pltpu.VMEM((128, 512), F32),
        pltpu.VMEM((16, 512), F32), pltpu.VMEM((4, 8, 128), F32),
        pltpu.VMEM((512, 512), F32), pltpu.VMEM((160, 512), F32), pltpu.VMEM((160, 512), F32),
        pltpu.VMEM((2, 512, 128), F32),
        pltpu.VMEM((1024, 1024), BF16), pltpu.VMEM((2, 512, 256), BF16),
        pltpu.VMEM((2, 256, 128), BF16), pltpu.VMEM((2, 128, 128), BF16),
        pltpu.VMEM((1024, FIB), BF16), pltpu.VMEM((7 * 256 + 16, FIB), BF16), pltpu.VMEM((128, FIB), BF16),
        pltpu.VMEM((128, 1024), BF16), pltpu.VMEM((4, 128, FIB), F32),
        *[pltpu.VMEM((2, 7 * n + 8, 128), F32) for n in NODES[::-1]],
        *[pltpu.VMEM((7 * n + 8, 128), F32) for n in NODES[::-1]],
        *[pltpu.VMEM((2, 4 * n, 128), F32) for n in NODES[::-1]],
        *[pltpu.VMEM((4 * n, 128), F32) for n in NODES[::-1]],
        pltpu.VMEM((8, 1024), F32), pltpu.VMEM((8, 1024), F32),
        pltpu.VMEM((16, 8, 128), F32), pltpu.VMEM((32, 8, 128), F32), pltpu.VMEM((16, 8, 128), F32),
        pltpu.VMEM((2, 40, 128), F32),
        dma, dma((6,)), dma, dma((3,)), dma((5, 2)), dma((8,)), dma((8,)), dma((5, 2)),
        dma((3, 7)), dma((3, 7)), dma((4,)), dma((4,)), dma((4,)), dma((4,)),
        dma, dma, dma, dma, dma, dma,
    ]
    bucket = bucket.reshape(1, FIB)
    solved, moving = pl.pallas_call(
        kernel,
        out_shape=(jax.ShapeDtypeStruct((4, 128, FIB), F32), jax.ShapeDtypeStruct((8, FIB), F32)),
        in_specs=[hbm] * 8,
        out_specs=(hbm, vmem),
        scratch_shapes=scratch,
        compiler_params=pltpu.CompilerParams(
            collective_id=0, has_side_effects=True, vmem_limit_bytes=60 * 2**20
        ),
    )(
        rhs, offsets, lengths.reshape(1, FIB), bucket, attach.reshape(1, FIB), operator, inverse, mobility,
    )

    def nodes(rows):
        return pl.BlockSpec((rows, 64, FIB), lambda i: (0, i, 0))

    return pl.pallas_call(
        add_motion,
        grid=(2,),
        out_shape=jax.ShapeDtypeStruct((4, 128, FIB), F32),
        in_specs=[
            nodes(4), nodes(3), pl.BlockSpec((8, FIB), lambda i: (0, 0)), pl.BlockSpec((1, FIB), lambda i: (0, 0)),
        ],
        out_specs=nodes(4),
        compiler_params=pltpu.CompilerParams(vmem_limit_bytes=60 * 2**20),
    )(solved, offsets, moving, bucket)


def solution(mesh):
    both = ("gx", "gy")
    in_specs = (
        P(None, None, both), P(None, None, both), P(both), P(both, None), P(both),
        P("gx", None, None), P("gx", None, None), P(None, both),
    )
    return jax.shard_map(body, mesh=mesh, in_specs=in_specs, out_specs=P(None, None, both), check_vma=False)
```
